32 devices in a mesh: ctx: 8 (over z, y), exp: 4 (over x, core).
Axes of the slice: x: 2, y: 2, z: 4, core: 2. Of those that a mesh axis runs over, the one named last changes fastest.
Arguments:
- scan_grad: bfloat16 [2048, 8192], P('ctx', 'exp'), may hold values from -6 to 6
- step_size: bfloat16 [2048, 8192], P('ctx', 'exp'), may hold values from 0.3 to 4.5, as said below
- scan_input: bfloat16 [2048, 8192], P('ctx', 'exp'), may hold values from -6 to 6
- state_in: float32 [2048, 16], P('ctx'), may hold values from -2 to 2
- state_out: float32 [2048, 16], P('ctx'), may hold values from -0.5 to 0.5
- decay_rate: float32 [16, 8192], P(None, 'exp'), may hold values from -1 to 0, as said below
- skip_gain: float32 [8192], P('exp'), may hold values from 0.5 to 1.5
Outputs:
- scan_input_grad: bfloat16 [2048, 8192], P('ctx', 'exp')
- state_in_grad: float32 [16, 2048], P(None, ('ctx', 'exp'))
The draws below stay inside these ranges and needn't reach their ends.
Inputs may be any that keep to these rules, and one draw needn't show every extreme that they name: `step_size`: Positive. `decay_rate`: Negative.
All inputs are finite; a program needn't handle non-finite values.
Results may differ from the reference program's by a relative error of at most 0.0015.
Values sent between devices are 32-bit elements; how exact they have to be, the bound alone decides.
A program may use at most 64 MiB of HBM per device.

```python
import math
import jax
import jax.numpy as jnp
from jax import lax

INNER = 8192
STATE = 16
TOK_DEV = 256
TOKENS = 2048


def draw_step_size(key, part):
    base_key, block_key, mixed_key = jax.random.split(key, 3)
    base = jax.random.uniform(base_key, (TOKENS, INNER), jnp.float32, 0.5, 1.5)
    factor = jnp.exp(jax.random.uniform(block_key, (TOKENS // TOK_DEV, 1, 1), jnp.float32, 0.0, math.log(3.0)))
    mixed = jnp.exp(jax.random.uniform(mixed_key, (TOKENS // TOK_DEV, 1, INNER), jnp.float32, -math.log(3.0), math.log(3.0)))
    shaped = base.reshape(TOKENS // TOK_DEV, TOK_DEV, INNER) * factor * mixed
    shaped = jnp.clip(shaped, 0.3, 4.5)
    return shaped.reshape(TOKENS, INNER).astype(jnp.bfloat16)


def draw_decay_rate(key, part):
    keys = jax.random.split(key, 5)
    spread = jnp.exp(jax.random.uniform(keys[0], (STATE, INNER), jnp.float32, 0.0, math.log(4.0)))
    fast_rate = jnp.exp(jax.random.uniform(keys[1], (1, INNER), jnp.float32, math.log(1.0 / 160.0), math.log(1.0 / 40.0)))
    slow_rate = jnp.exp(jax.random.uniform(keys[2], (1, INNER), jnp.float32, math.log(0.005), math.log(0.05))) / TOKENS
    middle_rate = jnp.exp(jax.random.uniform(keys[4], (1, INNER), jnp.float32, math.log(0.05), math.log(0.5))) / TOK_DEV
    chooser = jax.random.uniform(keys[3], (1, INNER), jnp.float32, 0.0, 1.0)
    fast_cut = 0.4
    middle_cut = 0.6
    picked = jnp.where(chooser < fast_cut, fast_rate, jnp.where(chooser < middle_cut, middle_rate, slow_rate))
    return -(picked * spread)


def block_levels(stream_key, shape, pieces, low, largest):
    gain = 1.0
    for axis_at, parts in pieces:
        draws = jax.random.uniform(jax.random.fold_in(jax.random.fold_in(stream_key, 6), axis_at), (parts,), jnp.float32, low / len(pieces), largest / len(pieces))
        gain = gain * jnp.repeat(jnp.exp(draws), shape[axis_at] // parts).reshape((-1,) + (1,) * (len(shape) - 1 - axis_at))
    return gain


def scatter_about(key, extent, width, reach, cuts=(), dtype=jnp.bfloat16):
    values = width * jax.random.normal(key, extent, jnp.float32)
    if cuts:
        values = values * block_levels(key, extent, cuts, -0.22, 0.18)
    return jnp.clip(values, -reach, reach).astype(dtype)


def setup_inputs(seed: int = 0) -> dict:
    key_list = jax.random.split(jax.random.key(seed), 8)
    scan_grad = scatter_about(key_list[0], (TOKENS, INNER), 1.0, 6.0, ((0, 8), (1, 4)))
    step_size = draw_step_size(jax.random.fold_in(key_list[7], 71), 0)
    scan_input = scatter_about(key_list[2], (TOKENS, INNER), 1.0, 6.0, ((0, 8), (1, 4)))
    state_in = scatter_about(key_list[3], (TOKENS, STATE), 0.125, 2.0, ((0, 8),), jnp.float32)
    state_out = scatter_about(key_list[4], (TOKENS, STATE), 0.03125, 0.5, ((0, 8),), jnp.float32)
    decay_rate = draw_decay_rate(jax.random.fold_in(key_list[7], 71), 0)
    skip_gain = jnp.clip(1.0 + 0.1 * jax.random.normal(key_list[6], (INNER,), jnp.float32), 0.5, 1.5)
    return dict(scan_grad=scan_grad, step_size=step_size, scan_input=scan_input, state_in=state_in, state_out=state_out, decay_rate=decay_rate, skip_gain=skip_gain)


def reference(scan_grad, step_size, scan_input, state_in, state_out, decay_rate, skip_gain):

    def step_back(incoming, row_data):
        grad_row, step_row, input_row, in_row, out_row = row_data
        grad_row = grad_row.astype(jnp.float32)
        step_row = step_row.astype(jnp.float32)
        input_row = input_row.astype(jnp.float32)
        adjoint = out_row[:, None] * grad_row[None, :] + incoming
        result = step_row * lax.optimization_barrier(jnp.sum(in_row[:, None] * adjoint, axis=0)) + skip_gain * grad_row
        b_grad = lax.optimization_barrier(jnp.sum(adjoint * (step_row * input_row)[None, :], axis=1))
        return (jnp.exp(step_row[None, :] * decay_rate) * adjoint, (result.astype(jnp.bfloat16), b_grad))
    start_state = jnp.zeros((STATE, INNER), jnp.float32)
    _, outputs = lax.scan(step_back, start_state, (scan_grad, step_size, scan_input, state_in, state_out), reverse=True)
    grads_all, b_all = outputs
    state_in_grad = jnp.transpose(b_all) * (1.0 / math.sqrt(INNER))
    return (grads_all, state_in_grad)
```

```python
import functools
import math

import jax
import jax.numpy as jnp
from jax import lax
from jax.experimental import pallas as pl
from jax.experimental.pallas import tpu as pltpu
from jax.sharding import PartitionSpec as P

MESH = pl.DeviceIdType.MESH
LANES = 128
TILES = 4
BLOCK = 16
LOG2E = math.log2(math.e)


def kernel(
    n_ctx, n_exp, scale,
    grad_hbm, step_hbm, input_hbm, in_ref, out_ref, rate_ref, gain_ref,
    dx_hbm, db_ref,
    grad_bf, step_bf, input_bf, dx_bf,
    grad_f, step_f, x_f, in_rep, out_rep, partial, transposer, rate2,
    summary, got_a, window, got_b, incoming_e, keep, give, got_c,
    share, got_share,
    load_sem, store_sem, a_sem, b_sem, c_sem, r_sem,
):
    rows, channels = grad_bf.shape[0], grad_hbm.shape[1]
    states = rate_ref.shape[0]
    width = TILES * LANES
    half = width // 2
    groups = channels // width
    blocks = rows // BLOCK
    section = rows // n_exp
    pairs = n_ctx // 2
    hops = []
    while (1 << len(hops)) < pairs:
        hops.append(1 << len(hops))

    ctx, me = lax.axis_index("ctx"), lax.axis_index("exp")
    side = lax.rem(ctx, 2)
    pair = ctx // 2
    partner = ctx + 1 - 2 * side
    low = side == 0

    def load(which, g):
        hbm, vmem = ((step_hbm, step_bf), (grad_hbm, grad_bf), (input_hbm, input_bf))[which]
        cols = pl.ds(g * width, width)
        return pltpu.make_async_copy(hbm.at[:, cols], vmem.at[:, cols], load_sem.at[which, g])

    for g in range(groups):
        load(0, g).start()
        load(1, g).start()
    for g in range(groups):
        load(2, g).start()

    barrier = pltpu.get_barrier_semaphore()
    count = 1 + (n_exp - 1)
    pl.semaphore_signal(barrier, inc=1, device_id=(partner, me), device_id_type=MESH)
    for other in range(1, n_exp):
        pl.semaphore_signal(
            barrier, inc=1, device_id=(ctx, lax.rem(me + other, n_exp)), device_id_type=MESH
        )
    for hop in hops:

        @pl.when(pair + hop < pairs)
        def _():
            pl.semaphore_signal(barrier, inc=1, device_id=(ctx + 2 * hop, me), device_id_type=MESH)

        @pl.when(pair >= hop)
        def _():
            pl.semaphore_signal(barrier, inc=1, device_id=(ctx - 2 * hop, me), device_id_type=MESH)

        count = count + jnp.where(pair + hop < pairs, 1, 0) + jnp.where(pair >= hop, 1, 0)

    for source, target in ((out_ref, out_rep), (in_ref, in_rep)):
        for start in range(0, rows, LANES):
            turned = jnp.transpose(source[start : start + LANES, :])
            for lane in range(LANES):
                target[start + lane] = jnp.broadcast_to(
                    turned[:, lane : lane + 1], (states, LANES)
                )
    for g in range(groups):
        for h in range(2):
            at = g * width + h * half
            rate2[g, h] = rate_ref[:, at : at + half] * LOG2E

    def rates(g):
        per_half = TILES // 2
        return [
            rate2[g, w // per_half, :, (w % per_half) * LANES : (w % per_half + 1) * LANES]
            for w in range(TILES)
        ]

    def columns(g, w):
        return pl.ds(g * width + w * LANES, LANES)

    def first_sweep(g):
        load(0, g).wait()
        load(1, g).wait()
        cols = pl.ds(g * width, width)

        def widen(b, total):
            at = pl.ds(pl.multiple_of(b * BLOCK, BLOCK), BLOCK)
            step = step_bf[at, cols].astype(jnp.float32)
            grad = grad_bf[at, cols].astype(jnp.float32)
            for k in range(BLOCK // 8):
                step_f[b * (BLOCK // 8) + k, :, cols] = step[8 * k : 8 * k + 8]
                grad_f[b * (BLOCK // 8) + k, :, cols] = grad[8 * k : 8 * k + 8]
                total = total + step[8 * k : 8 * k + 8]
            return total

        total = lax.fori_loop(0, blocks, widen, jnp.zeros((8, width), jnp.float32))
        rate = rates(g)

        def sweep(k, carry):
            carry = list(carry)
            b = blocks - 1 - k
            for i in range(BLOCK - 1, -1, -1):
                tile, sub = b * (BLOCK // 8) + i // 8, i % 8
                out = out_rep[b * BLOCK + i]
                for w in range(TILES):
                    step = step_f[tile, sub : sub + 1, columns(g, w)]
                    grad = grad_f[tile, sub : sub + 1, columns(g, w)]
                    carry[w] = jnp.exp2(step * rate[w]) * (out * grad + carry[w])
            return tuple(carry)

        zero = jnp.zeros((states, LANES), jnp.float32)
        carry = lax.fori_loop(0, blocks, sweep, (zero,) * TILES)
        reach = jnp.broadcast_to(jnp.sum(total, axis=0, keepdims=True), (8, width))
        per_half = TILES // 2
        for w in range(TILES):
            lanes = slice((w % per_half) * LANES, (w % per_half + 1) * LANES)
            summary[g, w // per_half, :states, lanes] = carry[w]
        for h in range(2):
            summary[g, h, states:, :] = reach[:, h * half : (h + 1) * half]

    def copy_a(g):
        return pltpu.make_async_remote_copy(
            src_ref=summary.at[g, 1 - side], dst_ref=got_a.at[g],
            send_sem=a_sem.at[0, g], recv_sem=a_sem.at[1, g],
            device_id=(partner, me), device_id_type=MESH,
        )

    def copy_b(g, k):
        return pltpu.make_async_remote_copy(
            src_ref=window.at[g, k], dst_ref=got_b.at[g, k],
            send_sem=b_sem.at[0, g, k], recv_sem=b_sem.at[1, g, k],
            device_id=(ctx - 2 * hops[k], me), device_id_type=MESH,
        )

    def copy_c(g):
        return pltpu.make_async_remote_copy(
            src_ref=give.at[g], dst_ref=got_c.at[g],
            send_sem=c_sem.at[0, g], recv_sem=c_sem.at[1, g],
            device_id=(partner, me), device_id_type=MESH,
        )

    def both_sides(g):
        own, other = summary[g, side], got_a[g]
        return jnp.where(low, own, other), jnp.where(low, other, own)

    def decay(rate, reach):
        return jnp.exp2(rate * jnp.concatenate([reach] * (states // 8), axis=0))

    def send_b(g, k):
        @pl.when(pair >= hops[k])
        def _():
            copy_b(g, k).start()

    def finish(g):
        first, second = both_sides(g)
        entering = incoming_e[g, :states]
        low_value = second[:states] + decay(rate2[g, side], second[states:]) * entering
        keep[g] = jnp.where(low, low_value, entering)
        give[g] = jnp.where(low, entering, low_value)
        copy_c(g).start()

    def stage(g, s):
        if s == 0:
            copy_a(g).start()
            return
        if s == 1:
            copy_a(g).wait_recv()
            first, second = both_sides(g)
            rate = rate2[g, side]
            window[g, 0, :states] = first[:states] + decay(rate, first[states:]) * second[:states]
            window[g, 0, states:] = first[states:] + second[states:]
            incoming_e[g] = jnp.zeros((states + 8, half), jnp.float32)
            if hops:
                send_b(g, 0)
            else:
                finish(g)
            return
        k = s - 2
        rate = rate2[g, side]

        @pl.when(pair + hops[k] < pairs)
        def _():
            copy_b(g, k).wait_recv()
            entering, got = incoming_e[g], got_b[g, k]
            incoming_e[g, :states] = (
                entering[:states] + decay(rate, entering[states:]) * got[:states]
            )
            incoming_e[g, states:] = entering[states:] + got[states:]

        if k + 1 < len(hops):
            mine, entering = window[g, 0], incoming_e[g]
            window[g, k + 1, :states] = (
                mine[:states] + decay(rate, mine[states:]) * entering[:states]
            )
            window[g, k + 1, states:] = mine[states:] + entering[states:]
            send_b(g, k + 1)
        else:
            finish(g)

    stages = 2 + len(hops)
    done = [0] * groups

    def advance(g, limit):
        while done[g] < min(limit, stages):
            stage(g, done[g])
            done[g] += 1

    lane_index = lax.broadcasted_iota(jnp.int32, (states, LANES), 1)

    def second_sweep(g):
        load(2, g).wait()
        cols = pl.ds(g * width, width)

        def widen(b, _):
            at = pl.ds(pl.multiple_of(b * BLOCK, BLOCK), BLOCK)
            part = input_bf[at, cols].astype(jnp.float32)
            for k in range(BLOCK // 8):
                tile = b * (BLOCK // 8) + k
                x_f[tile, :, cols] = part[8 * k : 8 * k + 8] * step_f[tile, :, cols]
            return 0

        lax.fori_loop(0, blocks, widen, 0)
        rate = rates(g)
        copy_c(g).wait_recv()
        mine, other = keep[g], got_c[g]
        halves = (jnp.where(low, mine, other), jnp.where(low, other, mine))
        per_half = TILES // 2
        carry = tuple(
            halves[w // per_half][:, (w % per_half) * LANES : (w % per_half + 1) * LANES]
            for w in range(TILES)
        )
        last = g == groups - 1
        gain = [gain_ref[:, columns(g, w)] for w in range(TILES)]

        def sweep(q, k, state):
            carry, sums = list(state[0]), state[1]
            per_section = section // BLOCK
            b = (q + 1) * per_section - 1 - k
            for i in range(BLOCK - 1, -1, -1):
                tile, sub = b * (BLOCK // 8) + i // 8, i % 8
                at = b * BLOCK + i
                out, inn = out_rep[at], in_rep[at]
                products = None
                for w in range(TILES):
                    step = step_f[tile, sub : sub + 1, columns(g, w)]
                    grad = grad_f[tile, sub : sub + 1, columns(g, w)]
                    x = x_f[tile, sub : sub + 1, columns(g, w)]
                    adjoint = out * grad + carry[w]
                    weighted = inn * adjoint
                    folded = weighted[:8]
                    for s in range(8, states, 8):
                        folded = folded + weighted[s : s + 8]
                    transposer[w, 8 * i : 8 * i + 8, :] = folded
                    product = adjoint * x
                    products = product if products is None else products + product
                    carry[w] = jnp.exp2(step * rate[w]) * adjoint
                if g > 0:
                    products = products + partial[at]
                if last:
                    summed = jnp.sum(products, axis=1, keepdims=True)
                    sums = jnp.where(lane_index == k_lane(b, i, q), summed, sums)
                else:
                    partial[at] = products
            for w in range(TILES):
                results = []
                for h in range(BLOCK // 8):
                    tile = b * (BLOCK // 8) + h
                    total = transposer[w, pl.ds(64 * h, 8, stride=8), :]
                    for s in range(1, 8):
                        total = total + transposer[w, pl.ds(64 * h + s, 8, stride=8), :]
                    results.append(
                        step_f[tile, :, columns(g, w)] * total
                        + gain[w] * grad_f[tile, :, columns(g, w)]
                    )
                dx_bf[pl.ds(pl.multiple_of(b * BLOCK, BLOCK), BLOCK), columns(g, w)] = (
                    jnp.concatenate(results, axis=0).astype(jnp.bfloat16)
                )
            return tuple(carry), sums

        def k_lane(b, i, q):
            return b * BLOCK + i - q * section

        zero = jnp.zeros((states, LANES), jnp.float32)
        if last:
            for q in range(n_exp - 1, -1, -1):
                carry, sums = lax.fori_loop(
                    0, section // BLOCK, functools.partial(sweep, q), (carry, zero)
                )
                share[q] = sums * scale

                @pl.when(me != q)
                def _():
                    copy_share(q).start()
        else:

            def all_rows(k, state):
                carry, _ = sweep_any(k, state)
                return carry, state[1]

            def sweep_any(k, state):
                b = blocks - 1 - k
                per_section = section // BLOCK
                return sweep(n_exp - 1, (n_exp * per_section - 1) - b, state)

            carry, _ = lax.fori_loop(0, blocks, all_rows, (carry, jnp.zeros((8, LANES), jnp.float32)))
        store(g).start()

    def store(g):
        cols = pl.ds(g * width, width)
        return pltpu.make_async_copy(dx_bf.at[:, cols], dx_hbm.at[:, cols], store_sem.at[g])

    def copy_share(q):
        return pltpu.make_async_remote_copy(
            src_ref=share.at[q], dst_ref=got_share.at[me],
            send_sem=r_sem.at[0, q], recv_sem=r_sem.at[1, me],
            device_id=(ctx, q), device_id_type=MESH,
        )

    for g in range(groups):
        first_sweep(g)
        if g == 0:
            pl.semaphore_wait(barrier, count)
        advance(g, 1)
        for earlier in range(g - 1, -1, -1):
            advance(earlier, g - earlier + 1)
    for g in range(groups):
        for later in range(groups - 1, g, -1):
            advance(later, groups + g - later + 1)
        advance(g, stages)
        second_sweep(g)

    total = share[me]
    for q in range(n_exp):

        @pl.when(me != q)
        def _():
            pltpu.make_async_remote_copy(
                src_ref=share.at[q], dst_ref=got_share.at[q],
                send_sem=r_sem.at[0, q], recv_sem=r_sem.at[1, q],
                device_id=(ctx, q), device_id_type=MESH,
            ).wait_recv()

    for other in range(1, n_exp):
        total = total + got_share[lax.rem(me + other, n_exp)]
    db_ref[...] = total[:, :section]

    for q in range(n_exp):

        @pl.when(me != q)
        def _():
            copy_share(q).wait_send()

    for g in range(groups):
        store(g).wait()
        copy_a(g).wait_send()
        copy_c(g).wait_send()
        for k, hop in enumerate(hops):

            @pl.when(pair >= hop)
            def _():
                copy_b(g, k).wait_send()


def shards(scan_grad, step_size, scan_input, state_in, state_out, decay_rate, skip_gain):
    n_ctx, n_exp = lax.axis_size("ctx"), lax.axis_size("exp")
    rows, channels = scan_grad.shape
    states = state_in.shape[1]
    width = TILES * LANES
    groups, half = channels // width, width // 2
    hops = max(1, (n_ctx // 2 - 1).bit_length())
    f32, bf16 = jnp.float32, jnp.bfloat16
    any_spec = pl.BlockSpec(memory_space=pl.ANY)
    vmem = pl.BlockSpec(memory_space=pltpu.VMEM)
    work = rows * channels * states
    return pl.pallas_call(
        functools.partial(kernel, n_ctx, n_exp, 1.0 / math.sqrt(channels * n_exp)),
        out_shape=(
            jax.ShapeDtypeStruct((rows, channels), bf16),
            jax.ShapeDtypeStruct((states, rows // n_exp), f32),
        ),
        in_specs=[any_spec, any_spec, any_spec, vmem, vmem, vmem, vmem],
        out_specs=(any_spec, vmem),
        scratch_shapes=[
            pltpu.VMEM((rows, channels), bf16),
            pltpu.VMEM((rows, channels), bf16),
            pltpu.VMEM((rows, channels), bf16),
            pltpu.VMEM((rows, channels), bf16),
            pltpu.VMEM((rows // 8, 8, channels), f32),
            pltpu.VMEM((rows // 8, 8, channels), f32),
            pltpu.VMEM((rows // 8, 8, channels), f32),
            pltpu.VMEM((rows, states, LANES), f32),
            pltpu.VMEM((rows, states, LANES), f32),
            pltpu.VMEM((rows, states, LANES), f32),
            pltpu.VMEM((TILES, 8 * BLOCK, LANES), f32),
            pltpu.VMEM((groups, 2, states, half), f32),
            pltpu.VMEM((groups, 2, states + 8, half), f32),
            pltpu.VMEM((groups, states + 8, half), f32),
            pltpu.VMEM((groups, hops, states + 8, half), f32),
            pltpu.VMEM((groups, hops, states + 8, half), f32),
            pltpu.VMEM((groups, states + 8, half), f32),
            pltpu.VMEM((groups, states, half), f32),
            pltpu.VMEM((groups, states, half), f32),
            pltpu.VMEM((groups, states, half), f32),
            pltpu.VMEM((n_exp, states, LANES), f32),
            pltpu.VMEM((n_exp, states, LANES), f32),
            pltpu.SemaphoreType.DMA((3, groups)),
            pltpu.SemaphoreType.DMA((groups,)),
            pltpu.SemaphoreType.DMA((2, groups)),
            pltpu.SemaphoreType.DMA((2, groups, hops)),
            pltpu.SemaphoreType.DMA((2, groups)),
            pltpu.SemaphoreType.DMA((2, n_exp)),
        ],
        compiler_params=pltpu.CompilerParams(
            collective_id=0, has_side_effects=True, vmem_limit_bytes=48 * 1024 * 1024
        ),
        cost_estimate=pl.CostEstimate(
            flops=14 * work, bytes_accessed=8 * rows * channels, transcendentals=2 * work
        ),
    )(
        scan_grad, step_size, scan_input, state_in, state_out, decay_rate,
        skip_gain.reshape(1, channels),
    )


def solution(mesh):
    in_specs = (
        P("ctx", "exp"),
        P("ctx", "exp"),
        P("ctx", "exp"),
        P("ctx", None),
        P("ctx", None),
        P(None, "exp"),
        P("exp"),
    )
    out_specs = (P("ctx", "exp"), P(None, ("ctx", "exp")))
    return jax.shard_map(shards, mesh=mesh, in_specs=in_specs, out_specs=out_specs, check_vma=False)
```

```python
import functools
import math

import jax
import jax.numpy as jnp
from jax import lax
from jax.experimental import pallas as pl
from jax.experimental.pallas import tpu as pltpu
from jax.sharding import PartitionSpec as P

MESH = pl.DeviceIdType.MESH
LANES = 128
TILES = 4
BLOCK = 16
LOG2E = math.log2(math.e)


def kernel(
    n_ctx, n_exp, scale,
    grad_hbm, step_hbm, input_hbm, in_ref, out_ref, rate_ref, gain_ref,
    dx_hbm, db_ref,
    grad_bf, step_bf, input_bf, dx_bf,
    grad_f, step_f, x_f, in_rep, out_rep, partial, transposer, rate2,
    summary, got_a, window, got_b, incoming_e, keep, give, got_c,
    share, got_share,
    load_sem, store_sem, a_sem, b_sem, c_sem, r_sem,
):
    rows, channels = grad_bf.shape[0], grad_hbm.shape[1]
    states = rate_ref.shape[0]
    width = TILES * LANES
    half = width // 2
    groups = channels // width
    blocks = rows // BLOCK
    section = rows // n_exp
    pairs = n_ctx // 2
    hops = []
    while (1 << len(hops)) < pairs:
        hops.append(1 << len(hops))

    ctx, me = lax.axis_index("ctx"), lax.axis_index("exp")
    side = lax.rem(ctx, 2)
    pair = ctx // 2
    partner = ctx + 1 - 2 * side
    low = side == 0

    def load(which, g):
        hbm, vmem = ((step_hbm, step_bf), (grad_hbm, grad_bf), (input_hbm, input_bf))[which]
        cols = pl.ds(g * width, width)
        return pltpu.make_async_copy(hbm.at[:, cols], vmem.at[:, cols], load_sem.at[which, g])

    for g in range(groups):
        load(0, g).start()
        load(1, g).start()
    for g in range(groups):
        load(2, g).start()

    barrier = pltpu.get_barrier_semaphore()
    count = 1 + (n_exp - 1)
    pl.semaphore_signal(barrier, inc=1, device_id=(partner, me), device_id_type=MESH)
    for other in range(1, n_exp):
        pl.semaphore_signal(
            barrier, inc=1, device_id=(ctx, lax.rem(me + other, n_exp)), device_id_type=MESH
        )
    for hop in hops:

        @pl.when(pair + hop < pairs)
        def _():
            pl.semaphore_signal(barrier, inc=1, device_id=(ctx + 2 * hop, me), device_id_type=MESH)

        @pl.when(pair >= hop)
        def _():
            pl.semaphore_signal(barrier, inc=1, device_id=(ctx - 2 * hop, me), device_id_type=MESH)

        count = count + jnp.where(pair + hop < pairs, 1, 0) + jnp.where(pair >= hop, 1, 0)

    def repeat(source, target):
        for start in range(0, rows, LANES):
            turned = source[:, start : start + LANES]
            for lane in range(LANES):
                target[start + lane] = jnp.broadcast_to(
                    turned[:, lane : lane + 1], (states, LANES)
                )

    repeat(out_ref, out_rep)
    for g in range(groups):
        for h in range(2):
            at = g * width + h * half
            rate2[g, h] = rate_ref[:, at : at + half] * LOG2E

    def rates(g):
        per_half = TILES // 2
        return [
            rate2[g, w // per_half, :, (w % per_half) * LANES : (w % per_half + 1) * LANES]
            for w in range(TILES)
        ]

    def row(ref, at, tile, sub):
        once = ref[at, tile, pl.ds(sub, 8, stride=0), :]
        return jnp.concatenate([once] * (states // 8), axis=0)

    def columns(g, w):
        return pl.ds(g * width + w * LANES, LANES)

    def first_sweep(g):
        load(0, g).wait()
        load(1, g).wait()
        cols = pl.ds(g * width, width)

        def widen(b, total):
            block = pl.ds(pl.multiple_of(b * BLOCK, BLOCK), BLOCK)
            step = step_bf[block, cols].astype(jnp.float32)
            grad = grad_bf[block, cols].astype(jnp.float32)
            for k in range(BLOCK // 8):
                for w in range(TILES):
                    at, lanes = g * TILES + w, slice(w * LANES, (w + 1) * LANES)
                    step_f[at, b * (BLOCK // 8) + k] = step[8 * k : 8 * k + 8, lanes]
                    grad_f[at, b * (BLOCK // 8) + k] = grad[8 * k : 8 * k + 8, lanes]
                total = total + step[8 * k : 8 * k + 8]
            return total

        total = lax.fori_loop(0, blocks, widen, jnp.zeros((8, width), jnp.float32))
        rate = rates(g)

        def sweep(k, carry):
            carry = list(carry)
            b = blocks - 1 - k
            for i in range(BLOCK - 1, -1, -1):
                tile, sub = b * (BLOCK // 8) + i // 8, i % 8
                out = out_rep[b * BLOCK + i]
                for w in range(TILES):
                    step = row(step_f, g * TILES + w, tile, sub)
                    grad = row(grad_f, g * TILES + w, tile, sub)
                    carry[w] = jnp.exp2(step * rate[w]) * (out * grad + carry[w])
            return tuple(carry)

        zero = jnp.zeros((states, LANES), jnp.float32)
        carry = lax.fori_loop(0, blocks, sweep, (zero,) * TILES)
        reach = jnp.broadcast_to(jnp.sum(total, axis=0, keepdims=True), (8, width))
        per_half = TILES // 2
        for w in range(TILES):
            lanes = slice((w % per_half) * LANES, (w % per_half + 1) * LANES)
            summary[g, w // per_half, :states, lanes] = carry[w]
        for h in range(2):
            summary[g, h, states:, :] = reach[:, h * half : (h + 1) * half]

    def copy_a(g):
        return pltpu.make_async_remote_copy(
            src_ref=summary.at[g, 1 - side], dst_ref=got_a.at[g],
            send_sem=a_sem.at[0, g], recv_sem=a_sem.at[1, g],
            device_id=(partner, me), device_id_type=MESH,
        )

    def copy_b(g, k):
        return pltpu.make_async_remote_copy(
            src_ref=window.at[g, k], dst_ref=got_b.at[g, k],
            send_sem=b_sem.at[0, g, k], recv_sem=b_sem.at[1, g, k],
            device_id=(ctx - 2 * hops[k], me), device_id_type=MESH,
        )

    def copy_c(g):
        return pltpu.make_async_remote_copy(
            src_ref=give.at[g], dst_ref=got_c.at[g],
            send_sem=c_sem.at[0, g], recv_sem=c_sem.at[1, g],
            device_id=(partner, me), device_id_type=MESH,
        )

    def both_sides(g):
        own, other = summary[g, side], got_a[g]
        return jnp.where(low, own, other), jnp.where(low, other, own)

    def decay(rate, reach):
        return jnp.exp2(rate * jnp.concatenate([reach] * (states // 8), axis=0))

    def send_b(g, k):
        @pl.when(pair >= hops[k])
        def _():
            copy_b(g, k).start()

    def finish(g):
        first, second = both_sides(g)
        entering = incoming_e[g, :states]
        low_value = second[:states] + decay(rate2[g, side], second[states:]) * entering
        keep[g] = jnp.where(low, low_value, entering)
        give[g] = jnp.where(low, entering, low_value)
        copy_c(g).start()

    def stage(g, s):
        if s == 0:
            copy_a(g).start()
            return
        if s == 1:
            copy_a(g).wait_recv()
            first, second = both_sides(g)
            rate = rate2[g, side]
            window[g, 0, :states] = first[:states] + decay(rate, first[states:]) * second[:states]
            window[g, 0, states:] = first[states:] + second[states:]
            incoming_e[g] = jnp.zeros((states + 8, half), jnp.float32)
            if hops:
                send_b(g, 0)
            else:
                finish(g)
            return
        k = s - 2
        rate = rate2[g, side]

        @pl.when(pair + hops[k] < pairs)
        def _():
            copy_b(g, k).wait_recv()
            entering, got = incoming_e[g], got_b[g, k]
            incoming_e[g, :states] = (
                entering[:states] + decay(rate, entering[states:]) * got[:states]
            )
            incoming_e[g, states:] = entering[states:] + got[states:]

        if k + 1 < len(hops):
            mine, entering = window[g, 0], incoming_e[g]
            window[g, k + 1, :states] = (
                mine[:states] + decay(rate, mine[states:]) * entering[:states]
            )
            window[g, k + 1, states:] = mine[states:] + entering[states:]
            send_b(g, k + 1)
        else:
            finish(g)

    stages = 2 + len(hops)
    done = [0] * groups

    def advance(g, limit):
        while done[g] < min(limit, stages):
            stage(g, done[g])
            done[g] += 1

    lane_index = lax.broadcasted_iota(jnp.int32, (states, LANES), 1)

    def second_sweep(g):
        load(2, g).wait()
        cols = pl.ds(g * width, width)

        def widen(b, _):
            block = pl.ds(pl.multiple_of(b * BLOCK, BLOCK), BLOCK)
            part = input_bf[block, cols].astype(jnp.float32)
            for k in range(BLOCK // 8):
                tile = b * (BLOCK // 8) + k
                for w in range(TILES):
                    at, lanes = g * TILES + w, slice(w * LANES, (w + 1) * LANES)
                    x_f[at, tile] = part[8 * k : 8 * k + 8, lanes] * step_f[at, tile]
            return 0

        lax.fori_loop(0, blocks, widen, 0)
        rate = rates(g)
        copy_c(g).wait_recv()
        mine, other = keep[g], got_c[g]
        halves = (jnp.where(low, mine, other), jnp.where(low, other, mine))
        per_half = TILES // 2
        carry = tuple(
            halves[w // per_half][:, (w % per_half) * LANES : (w % per_half + 1) * LANES]
            for w in range(TILES)
        )
        last = g == groups - 1
        gain = [gain_ref[:, columns(g, w)] for w in range(TILES)]

        def sweep(q, k, state):
            carry, sums = list(state[0]), state[1]
            per_section = section // BLOCK
            b = (q + 1) * per_section - 1 - k
            for i in range(BLOCK - 1, -1, -1):
                tile, sub = b * (BLOCK // 8) + i // 8, i % 8
                at = b * BLOCK + i
                out, inn = out_rep[at], in_rep[at]
                products = None
                for w in range(TILES):
                    step = row(step_f, g * TILES + w, tile, sub)
                    grad = row(grad_f, g * TILES + w, tile, sub)
                    x = row(x_f, g * TILES + w, tile, sub)
                    adjoint = out * grad + carry[w]
                    weighted = inn * adjoint
                    folded = weighted[:8]
                    for s in range(8, states, 8):
                        folded = folded + weighted[s : s + 8]
                    transposer[w, 8 * i : 8 * i + 8, :] = folded
                    product = adjoint * x
                    products = product if products is None else products + product
                    carry[w] = jnp.exp2(step * rate[w]) * adjoint
                if g > 0:
                    products = products + partial[at]
                if last:
                    summed = jnp.sum(products, axis=1, keepdims=True)
                    sums = jnp.where(lane_index == k_lane(b, i, q), summed, sums)
                else:
                    partial[at] = products
            for w in range(TILES):
                results = []
                for h in range(BLOCK // 8):
                    tile = b * (BLOCK // 8) + h
                    total = transposer[w, pl.ds(64 * h, 8, stride=8), :]
                    for s in range(1, 8):
                        total = total + transposer[w, pl.ds(64 * h + s, 8, stride=8), :]
                    results.append(
                        step_f[g * TILES + w, tile] * total
                        + gain[w] * grad_f[g * TILES + w, tile]
                    )
                dx_bf[pl.ds(pl.multiple_of(b * BLOCK, BLOCK), BLOCK), columns(g, w)] = (
                    jnp.concatenate(results, axis=0).astype(jnp.bfloat16)
                )
            return tuple(carry), sums

        def k_lane(b, i, q):
            return b * BLOCK + i - q * section

        zero = jnp.zeros((states, LANES), jnp.float32)
        if last:
            for q in range(n_exp - 1, -1, -1):
                carry, sums = lax.fori_loop(
                    0, section // BLOCK, functools.partial(sweep, q), (carry, zero)
                )
                share[q] = sums * scale

                @pl.when(me != q)
                def _():
                    copy_share(q).start()
        else:

            def all_rows(k, state):
                carry, _ = sweep_any(k, state)
                return carry, state[1]

            def sweep_any(k, state):
                b = blocks - 1 - k
                per_section = section // BLOCK
                return sweep(n_exp - 1, (n_exp * per_section - 1) - b, state)

            carry, _ = lax.fori_loop(0, blocks, all_rows, (carry, jnp.zeros((8, LANES), jnp.float32)))
        store(g).start()

    def store(g):
        cols = pl.ds(g * width, width)
        return pltpu.make_async_copy(dx_bf.at[:, cols], dx_hbm.at[:, cols], store_sem.at[g])

    def copy_share(q):
        return pltpu.make_async_remote_copy(
            src_ref=share.at[q], dst_ref=got_share.at[me],
            send_sem=r_sem.at[0, q], recv_sem=r_sem.at[1, me],
            device_id=(ctx, q), device_id_type=MESH,
        )

    for g in range(groups):
        first_sweep(g)
        if g == 0:
            pl.semaphore_wait(barrier, count)
        advance(g, 1)
        for earlier in range(g - 1, -1, -1):
            advance(earlier, g - earlier + 1)
    repeat(in_ref, in_rep)
    for g in range(groups):
        for later in range(groups - 1, g, -1):
            advance(later, groups + g - later + 1)
        advance(g, stages)
        second_sweep(g)

    total = share[me]
    for q in range(n_exp):

        @pl.when(me != q)
        def _():
            pltpu.make_async_remote_copy(
                src_ref=share.at[q], dst_ref=got_share.at[q],
                send_sem=r_sem.at[0, q], recv_sem=r_sem.at[1, q],
                device_id=(ctx, q), device_id_type=MESH,
            ).wait_recv()

    for other in range(1, n_exp):
        total = total + got_share[lax.rem(me + other, n_exp)]
    db_ref[...] = total[:, :section]

    for q in range(n_exp):

        @pl.when(me != q)
        def _():
            copy_share(q).wait_send()

    for g in range(groups):
        store(g).wait()
        copy_a(g).wait_send()
        copy_c(g).wait_send()
        for k, hop in enumerate(hops):

            @pl.when(pair >= hop)
            def _():
                copy_b(g, k).wait_send()


def shards(scan_grad, step_size, scan_input, state_in, state_out, decay_rate, skip_gain):
    n_ctx, n_exp = lax.axis_size("ctx"), lax.axis_size("exp")
    rows, channels = scan_grad.shape
    states = state_in.shape[1]
    width = TILES * LANES
    groups, half = channels // width, width // 2
    hops = max(1, (n_ctx // 2 - 1).bit_length())
    f32, bf16 = jnp.float32, jnp.bfloat16
    any_spec = pl.BlockSpec(memory_space=pl.ANY)
    vmem = pl.BlockSpec(memory_space=pltpu.VMEM)
    work = rows * channels * states
    return pl.pallas_call(
        functools.partial(kernel, n_ctx, n_exp, 1.0 / math.sqrt(channels * n_exp)),
        out_shape=(
            jax.ShapeDtypeStruct((rows, channels), bf16),
            jax.ShapeDtypeStruct((states, rows // n_exp), f32),
        ),
        in_specs=[any_spec, any_spec, any_spec, vmem, vmem, vmem, vmem],
        out_specs=(any_spec, vmem),
        scratch_shapes=[
            pltpu.VMEM((rows, channels), bf16),
            pltpu.VMEM((rows, channels), bf16),
            pltpu.VMEM((rows, channels), bf16),
            pltpu.VMEM((rows, channels), bf16),
            pltpu.VMEM((channels // LANES, rows // 8, 8, LANES), f32),
            pltpu.VMEM((channels // LANES, rows // 8, 8, LANES), f32),
            pltpu.VMEM((channels // LANES, rows // 8, 8, LANES), f32),
            pltpu.VMEM((rows, states, LANES), f32),
            pltpu.VMEM((rows, states, LANES), f32),
            pltpu.VMEM((rows, states, LANES), f32),
            pltpu.VMEM((TILES, 8 * BLOCK, LANES), f32),
            pltpu.VMEM((groups, 2, states, half), f32),
            pltpu.VMEM((groups, 2, states + 8, half), f32),
            pltpu.VMEM((groups, states + 8, half), f32),
            pltpu.VMEM((groups, hops, states + 8, half), f32),
            pltpu.VMEM((groups, hops, states + 8, half), f32),
            pltpu.VMEM((groups, states + 8, half), f32),
            pltpu.VMEM((groups, states, half), f32),
            pltpu.VMEM((groups, states, half), f32),
            pltpu.VMEM((groups, states, half), f32),
            pltpu.VMEM((n_exp, states, LANES), f32),
            pltpu.VMEM((n_exp, states, LANES), f32),
            pltpu.SemaphoreType.DMA((3, groups)),
            pltpu.SemaphoreType.DMA((groups,)),
            pltpu.SemaphoreType.DMA((2, groups)),
            pltpu.SemaphoreType.DMA((2, groups, hops)),
            pltpu.SemaphoreType.DMA((2, groups)),
            pltpu.SemaphoreType.DMA((2, n_exp)),
        ],
        compiler_params=pltpu.CompilerParams(
            collective_id=0, has_side_effects=True, vmem_limit_bytes=64 * 1024 * 1024
        ),
        cost_estimate=pl.CostEstimate(
            flops=14 * work, bytes_accessed=8 * rows * channels, transcendentals=2 * work
        ),
    )(
        scan_grad, step_size, scan_input, state_in.T, state_out.T, decay_rate,
        skip_gain.reshape(1, channels),
    )


def solution(mesh):
    in_specs = (
        P("ctx", "exp"),
        P("ctx", "exp"),
        P("ctx", "exp"),
        P("ctx", None),
        P("ctx", None),
        P(None, "exp"),
        P("exp"),
    )
    out_specs = (P("ctx", "exp"), P(None, ("ctx", "exp")))
    return jax.shard_map(shards, mesh=mesh, in_specs=in_specs, out_specs=out_specs, check_vma=False)
```

```python
import functools
import math

import jax
import jax.numpy as jnp
from jax import lax
from jax.experimental import pallas as pl
from jax.experimental.pallas import tpu as pltpu
from jax.sharding import PartitionSpec as P

MESH = pl.DeviceIdType.MESH
LANES = 128
TILES = 4
BLOCK = 16
LOG2E = math.log2(math.e)


def kernel(
    n_ctx, n_exp, scale,
    grad_hbm, step_hbm, input_hbm, in_ref, out_ref, rate_ref, gain_ref,
    dx_hbm, db_ref,
    grad_bf, step_bf, input_bf, dx_bf,
    grad_f, step_f, x_f, in_rep, out_rep, partial, rate2,
    summary, got_a, window, got_b, incoming_e, keep, give, got_c,
    share, got_share,
    load_sem, store_sem, a_sem, b_sem, c_sem, r_sem,
):
    rows, channels = grad_bf.shape[0], grad_hbm.shape[1]
    states = rate_ref.shape[0]
    width = TILES * LANES
    half = width // 2
    groups = channels // width
    blocks = rows // BLOCK
    section = rows // n_exp
    pairs = n_ctx // 2
    hops = []
    while (1 << len(hops)) < pairs:
        hops.append(1 << len(hops))

    ctx, me = lax.axis_index("ctx"), lax.axis_index("exp")
    side = lax.rem(ctx, 2)
    pair = ctx // 2
    partner = ctx + 1 - 2 * side
    low = side == 0

    def load(which, g):
        hbm, vmem = ((step_hbm, step_bf), (grad_hbm, grad_bf), (input_hbm, input_bf))[which]
        cols = pl.ds(g * width, width)
        return pltpu.make_async_copy(hbm.at[:, cols], vmem.at[:, cols], load_sem.at[which, g])

    for g in range(groups):
        load(0, g).start()
        load(1, g).start()
    for g in range(groups):
        load(2, g).start()

    barrier = pltpu.get_barrier_semaphore()
    count = 1 + (n_exp - 1)
    pl.semaphore_signal(barrier, inc=1, device_id=(partner, me), device_id_type=MESH)
    for other in range(1, n_exp):
        pl.semaphore_signal(
            barrier, inc=1, device_id=(ctx, lax.rem(me + other, n_exp)), device_id_type=MESH
        )
    for hop in hops:

        @pl.when(pair + hop < pairs)
        def _():
            pl.semaphore_signal(barrier, inc=1, device_id=(ctx + 2 * hop, me), device_id_type=MESH)

        @pl.when(pair >= hop)
        def _():
            pl.semaphore_signal(barrier, inc=1, device_id=(ctx - 2 * hop, me), device_id_type=MESH)

        count = count + jnp.where(pair + hop < pairs, 1, 0) + jnp.where(pair >= hop, 1, 0)

    def repeat(source, target):
        for start in range(0, rows, LANES):
            turned = source[:, start : start + LANES]
            for lane in range(LANES):
                target[start + lane] = jnp.broadcast_to(
                    turned[:, lane : lane + 1], (states, LANES)
                )

    repeat(out_ref, out_rep)
    for g in range(groups):
        for h in range(2):
            at = g * width + h * half
            rate2[g, h] = rate_ref[:, at : at + half] * LOG2E

    def rates(g):
        per_half = TILES // 2
        return [
            rate2[g, w // per_half, :, (w % per_half) * LANES : (w % per_half + 1) * LANES]
            for w in range(TILES)
        ]

    def row(ref, at, tile, sub):
        once = ref[at, tile, pl.ds(sub, 8, stride=0), :]
        return jnp.concatenate([once] * (states // 8), axis=0)

    def columns(g, w):
        return pl.ds(g * width + w * LANES, LANES)

    def first_sweep(g):
        load(0, g).wait()
        load(1, g).wait()
        cols = pl.ds(g * width, width)

        def widen(b, total):
            block = pl.ds(pl.multiple_of(b * BLOCK, BLOCK), BLOCK)
            step = step_bf[block, cols].astype(jnp.float32)
            grad = grad_bf[block, cols].astype(jnp.float32)
            for k in range(BLOCK // 8):
                for w in range(TILES):
                    at, lanes = g * TILES + w, slice(w * LANES, (w + 1) * LANES)
                    step_f[at, b * (BLOCK // 8) + k] = step[8 * k : 8 * k + 8, lanes]
                    grad_f[at, b * (BLOCK // 8) + k] = grad[8 * k : 8 * k + 8, lanes]
                total = total + step[8 * k : 8 * k + 8]
            return total

        total = lax.fori_loop(0, blocks, widen, jnp.zeros((8, width), jnp.float32))
        rate = rates(g)

        def sweep(k, carry):
            carry = list(carry)
            b = blocks - 1 - k
            for i in range(BLOCK - 1, -1, -1):
                tile, sub = b * (BLOCK // 8) + i // 8, i % 8
                out = out_rep[b * BLOCK + i]
                for w in range(TILES):
                    step = row(step_f, g * TILES + w, tile, sub)
                    grad = row(grad_f, g * TILES + w, tile, sub)
                    carry[w] = jnp.exp2(step * rate[w]) * (out * grad + carry[w])
            return tuple(carry)

        zero = jnp.zeros((states, LANES), jnp.float32)
        carry = lax.fori_loop(0, blocks, sweep, (zero,) * TILES)
        reach = jnp.broadcast_to(jnp.sum(total, axis=0, keepdims=True), (8, width))
        per_half = TILES // 2
        for w in range(TILES):
            lanes = slice((w % per_half) * LANES, (w % per_half + 1) * LANES)
            summary[g, w // per_half, :states, lanes] = carry[w]
        for h in range(2):
            summary[g, h, states:, :] = reach[:, h * half : (h + 1) * half]

    def copy_a(g):
        return pltpu.make_async_remote_copy(
            src_ref=summary.at[g, 1 - side], dst_ref=got_a.at[g],
            send_sem=a_sem.at[0, g], recv_sem=a_sem.at[1, g],
            device_id=(partner, me), device_id_type=MESH,
        )

    def copy_b(g, k):
        return pltpu.make_async_remote_copy(
            src_ref=window.at[g, k], dst_ref=got_b.at[g, k],
            send_sem=b_sem.at[0, g, k], recv_sem=b_sem.at[1, g, k],
            device_id=(ctx - 2 * hops[k], me), device_id_type=MESH,
        )

    def copy_c(g):
        return pltpu.make_async_remote_copy(
            src_ref=give.at[g], dst_ref=got_c.at[g],
            send_sem=c_sem.at[0, g], recv_sem=c_sem.at[1, g],
            device_id=(partner, me), device_id_type=MESH,
        )

    def both_sides(g):
        own, other = summary[g, side], got_a[g]
        return jnp.where(low, own, other), jnp.where(low, other, own)

    def decay(rate, reach):
        return jnp.exp2(rate * jnp.concatenate([reach] * (states // 8), axis=0))

    def send_b(g, k):
        @pl.when(pair >= hops[k])
        def _():
            copy_b(g, k).start()

    def finish(g):
        first, second = both_sides(g)
        entering = incoming_e[g, :states]
        low_value = second[:states] + decay(rate2[g, side], second[states:]) * entering
        keep[g] = jnp.where(low, low_value, entering)
        give[g] = jnp.where(low, entering, low_value)
        copy_c(g).start()

    def stage(g, s):
        if s == 0:
            copy_a(g).start()
            return
        if s == 1:
            copy_a(g).wait_recv()
            first, second = both_sides(g)
            rate = rate2[g, side]
            window[g, 0, :states] = first[:states] + decay(rate, first[states:]) * second[:states]
            window[g, 0, states:] = first[states:] + second[states:]
            incoming_e[g] = jnp.zeros((states + 8, half), jnp.float32)
            if hops:
                send_b(g, 0)
            else:
                finish(g)
            return
        k = s - 2
        rate = rate2[g, side]

        @pl.when(pair + hops[k] < pairs)
        def _():
            copy_b(g, k).wait_recv()
            entering, got = incoming_e[g], got_b[g, k]
            incoming_e[g, :states] = (
                entering[:states] + decay(rate, entering[states:]) * got[:states]
            )
            incoming_e[g, states:] = entering[states:] + got[states:]

        if k + 1 < len(hops):
            mine, entering = window[g, 0], incoming_e[g]
            window[g, k + 1, :states] = (
                mine[:states] + decay(rate, mine[states:]) * entering[:states]
            )
            window[g, k + 1, states:] = mine[states:] + entering[states:]
            send_b(g, k + 1)
        else:
            finish(g)

    stages = 2 + len(hops)
    done = [0] * groups

    def advance(g, limit):
        while done[g] < min(limit, stages):
            stage(g, done[g])
            done[g] += 1

    sublane = lax.broadcasted_iota(jnp.int32, (8, LANES), 0)

    def merge(stack, level, value):
        if level < 3 and stack and stack[-1][0] == level:
            later = stack.pop()[1]
            first = (sublane // (1 << level)) % 2 == 0
            stay = jnp.where(first, value, later)
            move = jnp.where(first, later, value)
            merge(stack, level + 1, stay + pltpu.roll(move, 8 - (1 << level), 0))
        else:
            stack.append((level, value))

    lane_index = lax.broadcasted_iota(jnp.int32, (states, LANES), 1)

    def second_sweep(g):
        load(2, g).wait()
        cols = pl.ds(g * width, width)

        def widen(b, _):
            block = pl.ds(pl.multiple_of(b * BLOCK, BLOCK), BLOCK)
            part = input_bf[block, cols].astype(jnp.float32)
            for k in range(BLOCK // 8):
                tile = b * (BLOCK // 8) + k
                for w in range(TILES):
                    at, lanes = g * TILES + w, slice(w * LANES, (w + 1) * LANES)
                    x_f[at, tile] = part[8 * k : 8 * k + 8, lanes] * step_f[at, tile]
            return 0

        lax.fori_loop(0, blocks, widen, 0)
        rate = rates(g)
        copy_c(g).wait_recv()
        mine, other = keep[g], got_c[g]
        halves = (jnp.where(low, mine, other), jnp.where(low, other, mine))
        per_half = TILES // 2
        carry = tuple(
            halves[w // per_half][:, (w % per_half) * LANES : (w % per_half + 1) * LANES]
            for w in range(TILES)
        )
        last = g == groups - 1
        gain = [gain_ref[:, columns(g, w)] for w in range(TILES)]

        def sweep(q, k, state):
            carry, sums = list(state[0]), state[1]
            per_section = section // BLOCK
            b = (q + 1) * per_section - 1 - k
            stacks = [[] for _ in range(TILES)]
            for i in range(BLOCK - 1, -1, -1):
                tile, sub = b * (BLOCK // 8) + i // 8, i % 8
                at = b * BLOCK + i
                out, inn = out_rep[at], in_rep[at]
                products = None
                for w in range(TILES):
                    step = row(step_f, g * TILES + w, tile, sub)
                    grad = row(grad_f, g * TILES + w, tile, sub)
                    x = row(x_f, g * TILES + w, tile, sub)
                    adjoint = out * grad + carry[w]
                    weighted = inn * adjoint
                    folded = weighted[:8]
                    for s in range(8, states, 8):
                        folded = folded + weighted[s : s + 8]
                    merge(stacks[w], 0, folded)
                    product = adjoint * x
                    products = product if products is None else products + product
                    carry[w] = jnp.exp2(step * rate[w]) * adjoint
                if g > 0:
                    products = products + partial[at]
                if last:
                    summed = jnp.sum(products, axis=1, keepdims=True)
                    sums = jnp.where(lane_index == k_lane(b, i, q), summed, sums)
                else:
                    partial[at] = products
            for w in range(TILES):
                results = []
                for h in range(BLOCK // 8):
                    tile = b * (BLOCK // 8) + h
                    total = stacks[w][BLOCK // 8 - 1 - h][1]
                    results.append(
                        step_f[g * TILES + w, tile] * total
                        + gain[w] * grad_f[g * TILES + w, tile]
                    )
                dx_bf[pl.ds(pl.multiple_of(b * BLOCK, BLOCK), BLOCK), columns(g, w)] = (
                    jnp.concatenate(results, axis=0).astype(jnp.bfloat16)
                )
            return tuple(carry), sums

        def k_lane(b, i, q):
            return b * BLOCK + i - q * section

        zero = jnp.zeros((states, LANES), jnp.float32)
        if last:
            for q in range(n_exp - 1, -1, -1):
                carry, sums = lax.fori_loop(
                    0, section // BLOCK, functools.partial(sweep, q), (carry, zero)
                )
                share[q] = sums * scale

                @pl.when(me != q)
                def _():
                    copy_share(q).start()
        else:

            def all_rows(k, state):
                carry, _ = sweep_any(k, state)
                return carry, state[1]

            def sweep_any(k, state):
                b = blocks - 1 - k
                per_section = section // BLOCK
                return sweep(n_exp - 1, (n_exp * per_section - 1) - b, state)

            carry, _ = lax.fori_loop(0, blocks, all_rows, (carry, jnp.zeros((8, LANES), jnp.float32)))
        store(g).start()

    def store(g):
        cols = pl.ds(g * width, width)
        return pltpu.make_async_copy(dx_bf.at[:, cols], dx_hbm.at[:, cols], store_sem.at[g])

    def copy_share(q):
        return pltpu.make_async_remote_copy(
            src_ref=share.at[q], dst_ref=got_share.at[me],
            send_sem=r_sem.at[0, q], recv_sem=r_sem.at[1, me],
            device_id=(ctx, q), device_id_type=MESH,
        )

    for g in range(groups):
        first_sweep(g)
        if g == 0:
            pl.semaphore_wait(barrier, count)
        advance(g, 1)
        for earlier in range(g - 1, -1, -1):
            advance(earlier, g - earlier + 1)
    repeat(in_ref, in_rep)
    for g in range(groups):
        for later in range(groups - 1, g, -1):
            advance(later, groups + g - later + 1)
        advance(g, stages)
        second_sweep(g)

    total = share[me]
    for q in range(n_exp):

        @pl.when(me != q)
        def _():
            pltpu.make_async_remote_copy(
                src_ref=share.at[q], dst_ref=got_share.at[q],
                send_sem=r_sem.at[0, q], recv_sem=r_sem.at[1, q],
                device_id=(ctx, q), device_id_type=MESH,
            ).wait_recv()

    for other in range(1, n_exp):
        total = total + got_share[lax.rem(me + other, n_exp)]
    db_ref[...] = total[:, :section]

    for q in range(n_exp):

        @pl.when(me != q)
        def _():
            copy_share(q).wait_send()

    for g in range(groups):
        store(g).wait()
        copy_a(g).wait_send()
        copy_c(g).wait_send()
        for k, hop in enumerate(hops):

            @pl.when(pair >= hop)
            def _():
                copy_b(g, k).wait_send()


def shards(scan_grad, step_size, scan_input, state_in, state_out, decay_rate, skip_gain):
    n_ctx, n_exp = lax.axis_size("ctx"), lax.axis_size("exp")
    rows, channels = scan_grad.shape
    states = state_in.shape[1]
    width = TILES * LANES
    groups, half = channels // width, width // 2
    hops = max(1, (n_ctx // 2 - 1).bit_length())
    f32, bf16 = jnp.float32, jnp.bfloat16
    hbm = pl.BlockSpec(memory_space=pltpu.HBM)
    any_spec = pl.BlockSpec(memory_space=pl.ANY)
    vmem = pl.BlockSpec(memory_space=pltpu.VMEM)
    work = rows * channels * states
    return pl.pallas_call(
        functools.partial(kernel, n_ctx, n_exp, 1.0 / math.sqrt(channels * n_exp)),
        out_shape=(
            jax.ShapeDtypeStruct((rows, channels), bf16),
            jax.ShapeDtypeStruct((states, rows // n_exp), f32),
        ),
        in_specs=[hbm, hbm, hbm, vmem, vmem, vmem, vmem],
        out_specs=(any_spec, vmem),
        scratch_shapes=[
            pltpu.VMEM((rows, channels), bf16),
            pltpu.VMEM((rows, channels), bf16),
            pltpu.VMEM((rows, channels), bf16),
            pltpu.VMEM((rows, channels), bf16),
            pltpu.VMEM((channels // LANES, rows // 8, 8, LANES), f32),
            pltpu.VMEM((channels // LANES, rows // 8, 8, LANES), f32),
            pltpu.VMEM((channels // LANES, rows // 8, 8, LANES), f32),
            pltpu.VMEM((rows, states, LANES), f32),
            pltpu.VMEM((rows, states, LANES), f32),
            pltpu.VMEM((rows, states, LANES), f32),
            pltpu.VMEM((groups, 2, states, half), f32),
            pltpu.VMEM((groups, 2, states + 8, half), f32),
            pltpu.VMEM((groups, states + 8, half), f32),
            pltpu.VMEM((groups, hops, states + 8, half), f32),
            pltpu.VMEM((groups, hops, states + 8, half), f32),
            pltpu.VMEM((groups, states + 8, half), f32),
            pltpu.VMEM((groups, states, half), f32),
            pltpu.VMEM((groups, states, half), f32),
            pltpu.VMEM((groups, states, half), f32),
            pltpu.VMEM((n_exp, states, LANES), f32),
            pltpu.VMEM((n_exp, states, LANES), f32),
            pltpu.SemaphoreType.DMA((3, groups)),
            pltpu.SemaphoreType.DMA((groups,)),
            pltpu.SemaphoreType.DMA((2, groups)),
            pltpu.SemaphoreType.DMA((2, groups, hops)),
            pltpu.SemaphoreType.DMA((2, groups)),
            pltpu.SemaphoreType.DMA((2, n_exp)),
        ],
        compiler_params=pltpu.CompilerParams(
            collective_id=0, has_side_effects=True, vmem_limit_bytes=62 * 1024 * 1024
        ),
        cost_estimate=pl.CostEstimate(
            flops=14 * work, bytes_accessed=8 * rows * channels, transcendentals=2 * work
        ),
    )(
        scan_grad, step_size, scan_input, state_in.T, state_out.T, decay_rate,
        skip_gain.reshape(1, channels),
    )


def solution(mesh):
    in_specs = (
        P("ctx", "exp"),
        P("ctx", "exp"),
        P("ctx", "exp"),
        P("ctx", None),
        P("ctx", None),
        P(None, "exp"),
        P("exp"),
    )
    out_specs = (P("ctx", "exp"), P(None, ("ctx", "exp")))
    return jax.shard_map(shards, mesh=mesh, in_specs=in_specs, out_specs=out_specs, check_vma=False)
```

```python
import functools
import math

import jax
import jax.numpy as jnp
from jax import lax
from jax.experimental import pallas as pl
from jax.experimental.pallas import tpu as pltpu
from jax.sharding import PartitionSpec as P

MESH = pl.DeviceIdType.MESH
LANES = 128
TILES = 4
BLOCK = 16
LOG2E = math.log2(math.e)


def kernel(
    n_ctx, n_exp, scale,
    grad_hbm, step_hbm, input_hbm, in_ref, out_ref, rate_ref, gain_ref,
    dx_hbm, db_ref,
    grad_bf, step_bf, input_bf, dx_bf,
    grad_f, step_f, x_f, in_rep, out_rep, partial, transposer, decays, rate2,
    summary, got_a, window, got_b, incoming_e, keep, give, got_c,
    share, got_share,
    load_sem, store_sem, a_sem, b_sem, c_sem, r_sem,
):
    rows, channels = grad_bf.shape[0], grad_hbm.shape[1]
    states = rate_ref.shape[0]
    width = TILES * LANES
    half = width // 2
    groups = channels // width
    blocks = rows // BLOCK
    section = rows // n_exp
    pairs = n_ctx // 2
    hops = []
    while (1 << len(hops)) < pairs:
        hops.append(1 << len(hops))

    ctx, me = lax.axis_index("ctx"), lax.axis_index("exp")
    side = lax.rem(ctx, 2)
    pair = ctx // 2
    partner = ctx + 1 - 2 * side
    low = side == 0

    def load(which, g):
        hbm, vmem = ((step_hbm, step_bf), (grad_hbm, grad_bf), (input_hbm, input_bf))[which]
        cols = pl.ds(g * width, width)
        return pltpu.make_async_copy(hbm.at[:, cols], vmem.at[:, cols], load_sem.at[which, g])

    for g in range(groups):
        load(0, g).start()
        load(1, g).start()
    for g in range(groups):
        load(2, g).start()

    barrier = pltpu.get_barrier_semaphore()
    count = 1 + (n_exp - 1)
    pl.semaphore_signal(barrier, inc=1, device_id=(partner, me), device_id_type=MESH)
    for other in range(1, n_exp):
        pl.semaphore_signal(
            barrier, inc=1, device_id=(ctx, lax.rem(me + other, n_exp)), device_id_type=MESH
        )
    for hop in hops:

        @pl.when(pair + hop < pairs)
        def _():
            pl.semaphore_signal(barrier, inc=1, device_id=(ctx + 2 * hop, me), device_id_type=MESH)

        @pl.when(pair >= hop)
        def _():
            pl.semaphore_signal(barrier, inc=1, device_id=(ctx - 2 * hop, me), device_id_type=MESH)

        count = count + jnp.where(pair + hop < pairs, 1, 0) + jnp.where(pair >= hop, 1, 0)

    def repeat(source, target):
        for start in range(0, rows, LANES):
            turned = source[:, start : start + LANES]
            for lane in range(LANES):
                target[start + lane] = jnp.broadcast_to(
                    turned[:, lane : lane + 1], (states, LANES)
                )

    repeat(out_ref, out_rep)
    for g in range(groups):
        for h in range(2):
            at = g * width + h * half
            rate2[g, h] = rate_ref[:, at : at + half] * LOG2E

    def rates(g):
        per_half = TILES // 2
        return [
            rate2[g, w // per_half, :, (w % per_half) * LANES : (w % per_half + 1) * LANES]
            for w in range(TILES)
        ]

    def row(ref, at, tile, sub):
        once = ref[at, tile, pl.ds(sub, 8, stride=0), :]
        return jnp.concatenate([once] * (states // 8), axis=0)

    def columns(g, w):
        return pl.ds(g * width + w * LANES, LANES)

    def first_sweep(g):
        load(0, g).wait()
        load(1, g).wait()
        cols = pl.ds(g * width, width)

        def widen(b, total):
            block = pl.ds(pl.multiple_of(b * BLOCK, BLOCK), BLOCK)
            step = step_bf[block, cols].astype(jnp.float32)
            grad = grad_bf[block, cols].astype(jnp.float32)
            for k in range(BLOCK // 8):
                for w in range(TILES):
                    at, lanes = g * TILES + w, slice(w * LANES, (w + 1) * LANES)
                    step_f[at, b * (BLOCK // 8) + k] = step[8 * k : 8 * k + 8, lanes]
                    grad_f[at, b * (BLOCK // 8) + k] = grad[8 * k : 8 * k + 8, lanes]
                total = total + step[8 * k : 8 * k + 8]
            return total

        total = lax.fori_loop(0, blocks, widen, jnp.zeros((8, width), jnp.float32))
        rate = rates(g)

        def sweep(k, carry):
            carry = list(carry)
            b = blocks - 1 - k
            for i in range(BLOCK - 1, -1, -1):
                tile, sub = b * (BLOCK // 8) + i // 8, i % 8
                out = out_rep[b * BLOCK + i]
                for w in range(TILES):
                    step = row(step_f, g * TILES + w, tile, sub)
                    grad = row(grad_f, g * TILES + w, tile, sub)
                    factor = jnp.exp2(step * rate[w])
                    decays[g, b * BLOCK + i, :, w * LANES : (w + 1) * LANES] = factor
                    carry[w] = factor * (out * grad + carry[w])
            return tuple(carry)

        zero = jnp.zeros((states, LANES), jnp.float32)
        carry = lax.fori_loop(0, blocks, sweep, (zero,) * TILES)
        reach = jnp.broadcast_to(jnp.sum(total, axis=0, keepdims=True), (8, width))
        per_half = TILES // 2
        for w in range(TILES):
            lanes = slice((w % per_half) * LANES, (w % per_half + 1) * LANES)
            summary[g, w // per_half, :states, lanes] = carry[w]
        for h in range(2):
            summary[g, h, states:, :] = reach[:, h * half : (h + 1) * half]

    def copy_a(g):
        return pltpu.make_async_remote_copy(
            src_ref=summary.at[g, 1 - side], dst_ref=got_a.at[g],
            send_sem=a_sem.at[0, g], recv_sem=a_sem.at[1, g],
            device_id=(partner, me), device_id_type=MESH,
        )

    def copy_b(g, k):
        return pltpu.make_async_remote_copy(
            src_ref=window.at[g, k], dst_ref=got_b.at[g, k],
            send_sem=b_sem.at[0, g, k], recv_sem=b_sem.at[1, g, k],
            device_id=(ctx - 2 * hops[k], me), device_id_type=MESH,
        )

    def copy_c(g):
        return pltpu.make_async_remote_copy(
            src_ref=give.at[g], dst_ref=got_c.at[g],
            send_sem=c_sem.at[0, g], recv_sem=c_sem.at[1, g],
            device_id=(partner, me), device_id_type=MESH,
        )

    def both_sides(g):
        own, other = summary[g, side], got_a[g]
        return jnp.where(low, own, other), jnp.where(low, other, own)

    def decay(rate, reach):
        return jnp.exp2(rate * jnp.concatenate([reach] * (states // 8), axis=0))

    def send_b(g, k):
        @pl.when(pair >= hops[k])
        def _():
            copy_b(g, k).start()

    def finish(g):
        first, second = both_sides(g)
        entering = incoming_e[g, :states]
        low_value = second[:states] + decay(rate2[g, side], second[states:]) * entering
        keep[g] = jnp.where(low, low_value, entering)
        give[g] = jnp.where(low, entering, low_value)
        copy_c(g).start()

    def stage(g, s):
        if s == 0:
            copy_a(g).start()
            return
        if s == 1:
            copy_a(g).wait_recv()
            first, second = both_sides(g)
            rate = rate2[g, side]
            window[g, 0, :states] = first[:states] + decay(rate, first[states:]) * second[:states]
            window[g, 0, states:] = first[states:] + second[states:]
            incoming_e[g] = jnp.zeros((states + 8, half), jnp.float32)
            if hops:
                send_b(g, 0)
            else:
                finish(g)
            return
        k = s - 2
        rate = rate2[g, side]

        @pl.when(pair + hops[k] < pairs)
        def _():
            copy_b(g, k).wait_recv()
            entering, got = incoming_e[g], got_b[g, k]
            incoming_e[g, :states] = (
                entering[:states] + decay(rate, entering[states:]) * got[:states]
            )
            incoming_e[g, states:] = entering[states:] + got[states:]

        if k + 1 < len(hops):
            mine, entering = window[g, 0], incoming_e[g]
            window[g, k + 1, :states] = (
                mine[:states] + decay(rate, mine[states:]) * entering[:states]
            )
            window[g, k + 1, states:] = mine[states:] + entering[states:]
            send_b(g, k + 1)
        else:
            finish(g)

    stages = 2 + len(hops)
    done = [0] * groups

    def advance(g, limit):
        while done[g] < min(limit, stages):
            stage(g, done[g])
            done[g] += 1

    lane_index = lax.broadcasted_iota(jnp.int32, (states, LANES), 1)

    def second_sweep(g):
        load(2, g).wait()
        cols = pl.ds(g * width, width)

        def widen(b, _):
            block = pl.ds(pl.multiple_of(b * BLOCK, BLOCK), BLOCK)
            part = input_bf[block, cols].astype(jnp.float32)
            for k in range(BLOCK // 8):
                tile = b * (BLOCK // 8) + k
                for w in range(TILES):
                    at, lanes = g * TILES + w, slice(w * LANES, (w + 1) * LANES)
                    x_f[at, tile] = part[8 * k : 8 * k + 8, lanes] * step_f[at, tile]
            return 0

        lax.fori_loop(0, blocks, widen, 0)
        copy_c(g).wait_recv()
        mine, other = keep[g], got_c[g]
        halves = (jnp.where(low, mine, other), jnp.where(low, other, mine))
        per_half = TILES // 2
        carry = tuple(
            halves[w // per_half][:, (w % per_half) * LANES : (w % per_half + 1) * LANES]
            for w in range(TILES)
        )
        last = g == groups - 1
        gain = [gain_ref[:, columns(g, w)] for w in range(TILES)]

        def sweep(q, k, state):
            carry, sums = list(state[0]), state[1]
            per_section = section // BLOCK
            b = (q + 1) * per_section - 1 - k
            for i in range(BLOCK - 1, -1, -1):
                tile, sub = b * (BLOCK // 8) + i // 8, i % 8
                at = b * BLOCK + i
                out, inn = out_rep[at], in_rep[at]
                products = None
                for w in range(TILES):
                    grad = row(grad_f, g * TILES + w, tile, sub)
                    x = row(x_f, g * TILES + w, tile, sub)
                    adjoint = out * grad + carry[w]
                    weighted = inn * adjoint
                    folded = weighted[:8]
                    for s in range(8, states, 8):
                        folded = folded + weighted[s : s + 8]
                    transposer[w, 8 * i : 8 * i + 8, :] = folded
                    product = adjoint * x
                    products = product if products is None else products + product
                    carry[w] = decays[g, at, :, w * LANES : (w + 1) * LANES] * adjoint
                if g > 0:
                    products = products + partial[at]
                if last:
                    summed = jnp.sum(products, axis=1, keepdims=True)
                    sums = jnp.where(lane_index == k_lane(b, i, q), summed, sums)
                else:
                    partial[at] = products
            for w in range(TILES):
                results = []
                for h in range(BLOCK // 8):
                    tile = b * (BLOCK // 8) + h
                    total = transposer[w, pl.ds(64 * h, 8, stride=8), :]
                    for s in range(1, 8):
                        total = total + transposer[w, pl.ds(64 * h + s, 8, stride=8), :]
                    results.append(
                        step_f[g * TILES + w, tile] * total
                        + gain[w] * grad_f[g * TILES + w, tile]
                    )
                dx_bf[pl.ds(pl.multiple_of(b * BLOCK, BLOCK), BLOCK), columns(g, w)] = (
                    jnp.concatenate(results, axis=0).astype(jnp.bfloat16)
                )
            return tuple(carry), sums

        def k_lane(b, i, q):
            return b * BLOCK + i - q * section

        zero = jnp.zeros((states, LANES), jnp.float32)
        if last:
            for q in range(n_exp - 1, -1, -1):
                carry, sums = lax.fori_loop(
                    0, section // BLOCK, functools.partial(sweep, q), (carry, zero)
                )
                share[q] = sums * scale

                @pl.when(me != q)
                def _():
                    copy_share(q).start()
        else:

            def all_rows(k, state):
                carry, _ = sweep_any(k, state)
                return carry, state[1]

            def sweep_any(k, state):
                b = blocks - 1 - k
                per_section = section // BLOCK
                return sweep(n_exp - 1, (n_exp * per_section - 1) - b, state)

            carry, _ = lax.fori_loop(0, blocks, all_rows, (carry, jnp.zeros((8, LANES), jnp.float32)))
        store(g).start()

    def store(g):
        cols = pl.ds(g * width, width)
        return pltpu.make_async_copy(dx_bf.at[:, cols], dx_hbm.at[:, cols], store_sem.at[g])

    def copy_share(q):
        return pltpu.make_async_remote_copy(
            src_ref=share.at[q], dst_ref=got_share.at[me],
            send_sem=r_sem.at[0, q], recv_sem=r_sem.at[1, me],
            device_id=(ctx, q), device_id_type=MESH,
        )

    for g in range(groups):
        first_sweep(g)
        if g == 0:
            pl.semaphore_wait(barrier, count)
        advance(g, 1)
        for earlier in range(g - 1, -1, -1):
            advance(earlier, g - earlier + 1)
    repeat(in_ref, in_rep)
    for g in range(groups):
        for later in range(groups - 1, g, -1):
            advance(later, groups + g - later + 1)
        advance(g, stages)
        second_sweep(g)

    total = share[me]
    for q in range(n_exp):

        @pl.when(me != q)
        def _():
            pltpu.make_async_remote_copy(
                src_ref=share.at[q], dst_ref=got_share.at[q],
                send_sem=r_sem.at[0, q], recv_sem=r_sem.at[1, q],
                device_id=(ctx, q), device_id_type=MESH,
            ).wait_recv()

    for other in range(1, n_exp):
        total = total + got_share[lax.rem(me + other, n_exp)]
    db_ref[...] = total[:, :section]

    for q in range(n_exp):

        @pl.when(me != q)
        def _():
            copy_share(q).wait_send()

    for g in range(groups):
        store(g).wait()
        copy_a(g).wait_send()
        copy_c(g).wait_send()
        for k, hop in enumerate(hops):

            @pl.when(pair >= hop)
            def _():
                copy_b(g, k).wait_send()


def shards(scan_grad, step_size, scan_input, state_in, state_out, decay_rate, skip_gain):
    n_ctx, n_exp = lax.axis_size("ctx"), lax.axis_size("exp")
    rows, channels = scan_grad.shape
    states = state_in.shape[1]
    width = TILES * LANES
    groups, half = channels // width, width // 2
    hops = max(1, (n_ctx // 2 - 1).bit_length())
    f32, bf16 = jnp.float32, jnp.bfloat16
    any_spec = pl.BlockSpec(memory_space=pl.ANY)
    vmem = pl.BlockSpec(memory_space=pltpu.VMEM)
    work = rows * channels * states
    return pl.pallas_call(
        functools.partial(kernel, n_ctx, n_exp, 1.0 / math.sqrt(channels * n_exp)),
        out_shape=(
            jax.ShapeDtypeStruct((rows, channels), bf16),
            jax.ShapeDtypeStruct((states, rows // n_exp), f32),
        ),
        in_specs=[any_spec, any_spec, any_spec, vmem, vmem, vmem, vmem],
        out_specs=(any_spec, vmem),
        scratch_shapes=[
            pltpu.VMEM((rows, channels), bf16),
            pltpu.VMEM((rows, channels), bf16),
            pltpu.VMEM((rows, channels), bf16),
            pltpu.VMEM((rows, channels), bf16),
            pltpu.VMEM((channels // LANES, rows // 8, 8, LANES), f32),
            pltpu.VMEM((channels // LANES, rows // 8, 8, LANES), f32),
            pltpu.VMEM((channels // LANES, rows // 8, 8, LANES), f32),
            pltpu.VMEM((rows, states, LANES), f32),
            pltpu.VMEM((rows, states, LANES), f32),
            pltpu.VMEM((rows, states, LANES), f32),
            pltpu.VMEM((TILES, 8 * BLOCK, LANES), f32),
            pltpu.VMEM((groups, rows, states, width), f32),
            pltpu.VMEM((groups, 2, states, half), f32),
            pltpu.VMEM((groups, 2, states + 8, half), f32),
            pltpu.VMEM((groups, states + 8, half), f32),
            pltpu.VMEM((groups, hops, states + 8, half), f32),
            pltpu.VMEM((groups, hops, states + 8, half), f32),
            pltpu.VMEM((groups, states + 8, half), f32),
            pltpu.VMEM((groups, states, half), f32),
            pltpu.VMEM((groups, states, half), f32),
            pltpu.VMEM((groups, states, half), f32),
            pltpu.VMEM((n_exp, states, LANES), f32),
            pltpu.VMEM((n_exp, states, LANES), f32),
            pltpu.SemaphoreType.DMA((3, groups)),
            pltpu.SemaphoreType.DMA((groups,)),
            pltpu.SemaphoreType.DMA((2, groups)),
            pltpu.SemaphoreType.DMA((2, groups, hops)),
            pltpu.SemaphoreType.DMA((2, groups)),
            pltpu.SemaphoreType.DMA((2, n_exp)),
        ],
        compiler_params=pltpu.CompilerParams(
            collective_id=0, has_side_effects=True, vmem_limit_bytes=62 * 1024 * 1024
        ),
        cost_estimate=pl.CostEstimate(
            flops=14 * work, bytes_accessed=8 * rows * channels, transcendentals=2 * work
        ),
    )(
        scan_grad, step_size, scan_input, state_in.T, state_out.T, decay_rate,
        skip_gain.reshape(1, channels),
    )


def solution(mesh):
    in_specs = (
        P("ctx", "exp"),
        P("ctx", "exp"),
        P("ctx", "exp"),
        P("ctx", None),
        P("ctx", None),
        P(None, "exp"),
        P("exp"),
    )
    out_specs = (P("ctx", "exp"), P(None, ("ctx", "exp")))
    return jax.shard_map(shards, mesh=mesh, in_specs=in_specs, out_specs=out_specs, check_vma=False)
```

```python
import functools
import math

import jax
import jax.numpy as jnp
from jax import lax
from jax.experimental import pallas as pl
from jax.experimental.pallas import tpu as pltpu
from jax.sharding import PartitionSpec as P

MESH = pl.DeviceIdType.MESH
LANES = 128
TILES = 4
BLOCK = 16
FAN = 4
LOG2E = math.log2(math.e)


def steps_over(pairs):
    hops, hop = [], 1
    while hop < pairs:
        hops.append(hop)
        hop *= FAN
    return hops


def kernel(
    n_ctx, n_exp, scale,
    grad_hbm, step_hbm, input_hbm, in_ref, out_ref, rate_ref, gain_ref,
    dx_hbm, db_ref,
    grad_bf, step_bf, input_bf, dx_bf,
    grad_f, step_f, x_f, in_rep, out_rep, partial, transposer, decays, rate2,
    summary, got_a, window, got_b, incoming_e, keep, give, got_c,
    share, got_share,
    load_sem, store_sem, a_sem, b_sem, c_sem, r_sem,
):
    rows, channels = grad_bf.shape[0], grad_hbm.shape[1]
    states = rate_ref.shape[0]
    width = TILES * LANES
    half = width // 2
    groups = channels // width
    blocks = rows // BLOCK
    section = rows // n_exp
    pairs = n_ctx // 2
    hops = steps_over(pairs)
    distances = [j * hop for hop in hops for j in range(1, FAN)]

    ctx, me = lax.axis_index("ctx"), lax.axis_index("exp")
    side = lax.rem(ctx, 2)
    pair = ctx // 2
    partner = ctx + 1 - 2 * side
    low = side == 0

    def load(which, g):
        hbm, vmem = ((step_hbm, step_bf), (grad_hbm, grad_bf), (input_hbm, input_bf))[which]
        cols = pl.ds(g * width, width)
        return pltpu.make_async_copy(hbm.at[:, cols], vmem.at[:, cols], load_sem.at[which, g])

    for g in range(groups):
        load(0, g).start()
        load(1, g).start()
    for g in range(groups):
        load(2, g).start()

    barrier = pltpu.get_barrier_semaphore()
    count = 1 + (n_exp - 1)
    pl.semaphore_signal(barrier, inc=1, device_id=(partner, me), device_id_type=MESH)
    for other in range(1, n_exp):
        pl.semaphore_signal(
            barrier, inc=1, device_id=(ctx, lax.rem(me + other, n_exp)), device_id_type=MESH
        )
    for hop in distances:

        @pl.when(pair + hop < pairs)
        def _():
            pl.semaphore_signal(barrier, inc=1, device_id=(ctx + 2 * hop, me), device_id_type=MESH)

        @pl.when(pair >= hop)
        def _():
            pl.semaphore_signal(barrier, inc=1, device_id=(ctx - 2 * hop, me), device_id_type=MESH)

        count = count + jnp.where(pair + hop < pairs, 1, 0) + jnp.where(pair >= hop, 1, 0)

    def repeat(source, target):
        for start in range(0, rows, LANES):
            turned = source[:, start : start + LANES]
            for lane in range(LANES):
                target[start + lane] = jnp.broadcast_to(
                    turned[:, lane : lane + 1], (states, LANES)
                )

    repeat(out_ref, out_rep)
    for g in range(groups):
        for h in range(2):
            at = g * width + h * half
            rate2[g, h] = rate_ref[:, at : at + half] * LOG2E

    def rates(g):
        per_half = TILES // 2
        return [
            rate2[g, w // per_half, :, (w % per_half) * LANES : (w % per_half + 1) * LANES]
            for w in range(TILES)
        ]

    def row(ref, at, tile, sub):
        once = ref[at, tile, pl.ds(sub, 8, stride=0), :]
        return jnp.concatenate([once] * (states // 8), axis=0)

    def columns(g, w):
        return pl.ds(g * width + w * LANES, LANES)

    def first_sweep(g):
        load(0, g).wait()
        load(1, g).wait()
        cols = pl.ds(g * width, width)

        def widen(b, total):
            block = pl.ds(pl.multiple_of(b * BLOCK, BLOCK), BLOCK)
            step = step_bf[block, cols].astype(jnp.float32)
            grad = grad_bf[block, cols].astype(jnp.float32)
            for k in range(BLOCK // 8):
                for w in range(TILES):
                    at, lanes = g * TILES + w, slice(w * LANES, (w + 1) * LANES)
                    step_f[at, b * (BLOCK // 8) + k] = step[8 * k : 8 * k + 8, lanes]
                    grad_f[at, b * (BLOCK // 8) + k] = grad[8 * k : 8 * k + 8, lanes]
                total = total + step[8 * k : 8 * k + 8]
            return total

        total = lax.fori_loop(0, blocks, widen, jnp.zeros((8, width), jnp.float32))
        rate = rates(g)

        def sweep(k, carry):
            carry = list(carry)
            b = blocks - 1 - k
            for i in range(BLOCK - 1, -1, -1):
                tile, sub = b * (BLOCK // 8) + i // 8, i % 8
                out = out_rep[b * BLOCK + i]
                for w in range(TILES):
                    step = row(step_f, g * TILES + w, tile, sub)
                    grad = row(grad_f, g * TILES + w, tile, sub)
                    factor = jnp.exp2(step * rate[w])
                    decays[g, b * BLOCK + i, :, w * LANES : (w + 1) * LANES] = factor
                    carry[w] = factor * (out * grad + carry[w])
            return tuple(carry)

        zero = jnp.zeros((states, LANES), jnp.float32)
        carry = lax.fori_loop(0, blocks, sweep, (zero,) * TILES)
        reach = jnp.broadcast_to(jnp.sum(total, axis=0, keepdims=True), (8, width))
        per_half = TILES // 2
        for w in range(TILES):
            lanes = slice((w % per_half) * LANES, (w % per_half + 1) * LANES)
            summary[g, w // per_half, :states, lanes] = carry[w]
        for h in range(2):
            summary[g, h, states:, :] = reach[:, h * half : (h + 1) * half]

    def copy_a(g):
        return pltpu.make_async_remote_copy(
            src_ref=summary.at[g, 1 - side], dst_ref=got_a.at[g],
            send_sem=a_sem.at[0, g], recv_sem=a_sem.at[1, g],
            device_id=(partner, me), device_id_type=MESH,
        )

    def copy_b(g, k, j):
        slot = k * (FAN - 1) + j - 1
        return pltpu.make_async_remote_copy(
            src_ref=window.at[g, k], dst_ref=got_b.at[g, slot],
            send_sem=b_sem.at[0, g, slot], recv_sem=b_sem.at[1, g, slot],
            device_id=(ctx - 2 * j * hops[k], me), device_id_type=MESH,
        )

    def copy_c(g):
        return pltpu.make_async_remote_copy(
            src_ref=give.at[g], dst_ref=got_c.at[g],
            send_sem=c_sem.at[0, g], recv_sem=c_sem.at[1, g],
            device_id=(partner, me), device_id_type=MESH,
        )

    def both_sides(g):
        own, other = summary[g, side], got_a[g]
        return jnp.where(low, own, other), jnp.where(low, other, own)

    def decay(rate, reach):
        return jnp.exp2(rate * jnp.concatenate([reach] * (states // 8), axis=0))

    def send_b(g, k):
        for j in range(1, FAN):

            @pl.when(pair >= j * hops[k])
            def _():
                copy_b(g, k, j).start()

    def finish(g):
        first, second = both_sides(g)
        entering = incoming_e[g, :states]
        low_value = second[:states] + decay(rate2[g, side], second[states:]) * entering
        keep[g] = jnp.where(low, low_value, entering)
        give[g] = jnp.where(low, entering, low_value)
        copy_c(g).start()

    def stage(g, s):
        if s == 0:
            copy_a(g).start()
            return
        if s == 1:
            copy_a(g).wait_recv()
            first, second = both_sides(g)
            rate = rate2[g, side]
            window[g, 0, :states] = first[:states] + decay(rate, first[states:]) * second[:states]
            window[g, 0, states:] = first[states:] + second[states:]
            incoming_e[g] = jnp.zeros((states + 8, half), jnp.float32)
            if hops:
                send_b(g, 0)
            else:
                finish(g)
            return
        k = s - 2
        rate = rate2[g, side]

        for j in range(1, FAN):

            @pl.when(pair + j * hops[k] < pairs)
            def _():
                copy_b(g, k, j).wait_recv()
                entering, got = incoming_e[g], got_b[g, k * (FAN - 1) + j - 1]
                incoming_e[g, :states] = (
                    entering[:states] + decay(rate, entering[states:]) * got[:states]
                )
                incoming_e[g, states:] = entering[states:] + got[states:]

        if k + 1 < len(hops):
            mine, entering = window[g, 0], incoming_e[g]
            window[g, k + 1, :states] = (
                mine[:states] + decay(rate, mine[states:]) * entering[:states]
            )
            window[g, k + 1, states:] = mine[states:] + entering[states:]
            send_b(g, k + 1)
        else:
            finish(g)

    stages = 2 + len(hops)
    done = [0] * groups

    def advance(g, limit):
        while done[g] < min(limit, stages):
            stage(g, done[g])
            done[g] += 1

    lane_index = lax.broadcasted_iota(jnp.int32, (states, LANES), 1)

    def weigh_inputs(g):
        load(2, g).wait()
        cols = pl.ds(g * width, width)

        def widen(b, _):
            block = pl.ds(pl.multiple_of(b * BLOCK, BLOCK), BLOCK)
            part = input_bf[block, cols].astype(jnp.float32)
            for k in range(BLOCK // 8):
                tile = b * (BLOCK // 8) + k
                for w in range(TILES):
                    at, lanes = g * TILES + w, slice(w * LANES, (w + 1) * LANES)
                    x_f[at, tile] = part[8 * k : 8 * k + 8, lanes] * step_f[at, tile]
            return 0

        lax.fori_loop(0, blocks, widen, 0)

    def second_sweep(g):
        copy_c(g).wait_recv()
        mine, other = keep[g], got_c[g]
        halves = (jnp.where(low, mine, other), jnp.where(low, other, mine))
        per_half = TILES // 2
        carry = tuple(
            halves[w // per_half][:, (w % per_half) * LANES : (w % per_half + 1) * LANES]
            for w in range(TILES)
        )
        last = g == groups - 1
        gain = [gain_ref[:, columns(g, w)] for w in range(TILES)]

        def sweep(q, k, state):
            carry, sums = list(state[0]), state[1]
            per_section = section // BLOCK
            b = (q + 1) * per_section - 1 - k
            for i in range(BLOCK - 1, -1, -1):
                tile, sub = b * (BLOCK // 8) + i // 8, i % 8
                at = b * BLOCK + i
                out, inn = out_rep[at], in_rep[at]
                products = None
                for w in range(TILES):
                    grad = row(grad_f, g * TILES + w, tile, sub)
                    x = row(x_f, g * TILES + w, tile, sub)
                    adjoint = out * grad + carry[w]
                    weighted = inn * adjoint
                    folded = weighted[:8]
                    for s in range(8, states, 8):
                        folded = folded + weighted[s : s + 8]
                    transposer[w, 8 * i : 8 * i + 8, :] = folded
                    product = adjoint * x
                    products = product if products is None else products + product
                    carry[w] = decays[g, at, :, w * LANES : (w + 1) * LANES] * adjoint
                if g > 0:
                    products = products + partial[at]
                if last:
                    summed = jnp.sum(products, axis=1, keepdims=True)
                    sums = jnp.where(lane_index == k_lane(b, i, q), summed, sums)
                else:
                    partial[at] = products
            for w in range(TILES):
                results = []
                for h in range(BLOCK // 8):
                    tile = b * (BLOCK // 8) + h
                    total = transposer[w, pl.ds(64 * h, 8, stride=8), :]
                    for s in range(1, 8):
                        total = total + transposer[w, pl.ds(64 * h + s, 8, stride=8), :]
                    results.append(
                        step_f[g * TILES + w, tile] * total
                        + gain[w] * grad_f[g * TILES + w, tile]
                    )
                dx_bf[pl.ds(pl.multiple_of(b * BLOCK, BLOCK), BLOCK), columns(g, w)] = (
                    jnp.concatenate(results, axis=0).astype(jnp.bfloat16)
                )
            return tuple(carry), sums

        def k_lane(b, i, q):
            return b * BLOCK + i - q * section

        zero = jnp.zeros((states, LANES), jnp.float32)
        if last:
            for q in range(n_exp - 1, -1, -1):
                carry, sums = lax.fori_loop(
                    0, section // BLOCK, functools.partial(sweep, q), (carry, zero)
                )
                share[q] = sums * scale

                @pl.when(me != q)
                def _():
                    copy_share(q).start()
        else:

            def all_rows(k, state):
                carry, _ = sweep_any(k, state)
                return carry, state[1]

            def sweep_any(k, state):
                b = blocks - 1 - k
                per_section = section // BLOCK
                return sweep(n_exp - 1, (n_exp * per_section - 1) - b, state)

            carry, _ = lax.fori_loop(0, blocks, all_rows, (carry, jnp.zeros((8, LANES), jnp.float32)))
        store(g).start()

    def store(g):
        cols = pl.ds(g * width, width)
        return pltpu.make_async_copy(dx_bf.at[:, cols], dx_hbm.at[:, cols], store_sem.at[g])

    def copy_share(q):
        return pltpu.make_async_remote_copy(
            src_ref=share.at[q], dst_ref=got_share.at[me],
            send_sem=r_sem.at[0, q], recv_sem=r_sem.at[1, me],
            device_id=(ctx, q), device_id_type=MESH,
        )

    for g in range(groups):
        first_sweep(g)
        if g == 0:
            pl.semaphore_wait(barrier, count)
        advance(g, 1)
        if g >= 2:
            advance(g - 2, 2)
    repeat(in_ref, in_rep)
    advance(0, 3)
    for g in range(groups):
        weigh_inputs(g)
    for g in range(1, groups):
        advance(g, 2)
    advance(min(1, groups - 1), 3)
    for g in range(groups):
        for later in range(g, groups if g > 0 else 1):
            advance(later, stages)
        second_sweep(g)

    total = share[me]
    for q in range(n_exp):

        @pl.when(me != q)
        def _():
            pltpu.make_async_remote_copy(
                src_ref=share.at[q], dst_ref=got_share.at[q],
                send_sem=r_sem.at[0, q], recv_sem=r_sem.at[1, q],
                device_id=(ctx, q), device_id_type=MESH,
            ).wait_recv()

    for other in range(1, n_exp):
        total = total + got_share[lax.rem(me + other, n_exp)]
    db_ref[...] = total[:, :section]

    for q in range(n_exp):

        @pl.when(me != q)
        def _():
            copy_share(q).wait_send()

    for g in range(groups):
        store(g).wait()
        copy_a(g).wait_send()
        copy_c(g).wait_send()
        for k, hop in enumerate(hops):
            for j in range(1, FAN):

                @pl.when(pair >= j * hop)
                def _():
                    copy_b(g, k, j).wait_send()


def shards(scan_grad, step_size, scan_input, state_in, state_out, decay_rate, skip_gain):
    n_ctx, n_exp = lax.axis_size("ctx"), lax.axis_size("exp")
    rows, channels = scan_grad.shape
    states = state_in.shape[1]
    width = TILES * LANES
    groups, half = channels // width, width // 2
    hops = max(1, len(steps_over(n_ctx // 2)))
    slots = hops * (FAN - 1)
    f32, bf16 = jnp.float32, jnp.bfloat16
    any_spec = pl.BlockSpec(memory_space=pl.ANY)
    vmem = pl.BlockSpec(memory_space=pltpu.VMEM)
    work = rows * channels * states
    return pl.pallas_call(
        functools.partial(kernel, n_ctx, n_exp, 1.0 / math.sqrt(channels * n_exp)),
        out_shape=(
            jax.ShapeDtypeStruct((rows, channels), bf16),
            jax.ShapeDtypeStruct((states, rows // n_exp), f32),
        ),
        in_specs=[any_spec, any_spec, any_spec, vmem, vmem, vmem, vmem],
        out_specs=(any_spec, vmem),
        scratch_shapes=[
            pltpu.VMEM((rows, channels), bf16),
            pltpu.VMEM((rows, channels), bf16),
            pltpu.VMEM((rows, channels), bf16),
            pltpu.VMEM((rows, channels), bf16),
            pltpu.VMEM((channels // LANES, rows // 8, 8, LANES), f32),
            pltpu.VMEM((channels // LANES, rows // 8, 8, LANES), f32),
            pltpu.VMEM((channels // LANES, rows // 8, 8, LANES), f32),
            pltpu.VMEM((rows, states, LANES), f32),
            pltpu.VMEM((rows, states, LANES), f32),
            pltpu.VMEM((rows, states, LANES), f32),
            pltpu.VMEM((TILES, 8 * BLOCK, LANES), f32),
            pltpu.VMEM((groups, rows, states, width), f32),
            pltpu.VMEM((groups, 2, states, half), f32),
            pltpu.VMEM((groups, 2, states + 8, half), f32),
            pltpu.VMEM((groups, states + 8, half), f32),
            pltpu.VMEM((groups, hops, states + 8, half), f32),
            pltpu.VMEM((groups, slots, states + 8, half), f32),
            pltpu.VMEM((groups, states + 8, half), f32),
            pltpu.VMEM((groups, states, half), f32),
            pltpu.VMEM((groups, states, half), f32),
            pltpu.VMEM((groups, states, half), f32),
            pltpu.VMEM((n_exp, states, LANES), f32),
            pltpu.VMEM((n_exp, states, LANES), f32),
            pltpu.SemaphoreType.DMA((3, groups)),
            pltpu.SemaphoreType.DMA((groups,)),
            pltpu.SemaphoreType.DMA((2, groups)),
            pltpu.SemaphoreType.DMA((2, groups, slots)),
            pltpu.SemaphoreType.DMA((2, groups)),
            pltpu.SemaphoreType.DMA((2, n_exp)),
        ],
        compiler_params=pltpu.CompilerParams(
            collective_id=0, has_side_effects=True, vmem_limit_bytes=62 * 1024 * 1024
        ),
        cost_estimate=pl.CostEstimate(
            flops=14 * work, bytes_accessed=8 * rows * channels, transcendentals=2 * work
        ),
    )(
        scan_grad, step_size, scan_input, state_in.T, state_out.T, decay_rate,
        skip_gain.reshape(1, channels),
    )


def solution(mesh):
    in_specs = (
        P("ctx", "exp"),
        P("ctx", "exp"),
        P("ctx", "exp"),
        P("ctx", None),
        P("ctx", None),
        P(None, "exp"),
        P("exp"),
    )
    out_specs = (P("ctx", "exp"), P(None, ("ctx", "exp")))
    return jax.shard_map(shards, mesh=mesh, in_specs=in_specs, out_specs=out_specs, check_vma=False)
```

```python
import functools
import math

import jax
import jax.numpy as jnp
from jax import lax
from jax.experimental import pallas as pl
from jax.experimental.pallas import tpu as pltpu
from jax.sharding import PartitionSpec as P

MESH = pl.DeviceIdType.MESH
LANES = 128
TILES = 4
BLOCK = 32
WIDE = 128
FAN = 4
LOG2E = math.log2(math.e)


def steps_over(pairs):
    hops, hop = [], 1
    while hop < pairs:
        hops.append(hop)
        hop *= FAN
    return hops


def kernel(
    n_ctx, n_exp, scale,
    grad_hbm, step_hbm, input_hbm, in_ref, out_ref, rate_ref, gain_ref,
    dx_hbm, db_ref,
    grad_bf, step_bf, input_bf, dx_bf,
    grad_f, step_f, x_f, in_rep, out_rep, partial, transposer, decays, rate2,
    summary, got_a, window, got_b, incoming_e, keep, give, got_c,
    share, got_share,
    load_sem, store_sem, a_sem, b_sem, c_sem, r_sem,
):
    rows, channels = grad_bf.shape[0], grad_hbm.shape[1]
    states = rate_ref.shape[0]
    width = TILES * LANES
    half = width // 2
    groups = channels // width
    blocks = rows // BLOCK
    section = rows // n_exp
    pairs = n_ctx // 2
    hops = steps_over(pairs)
    distances = [j * hop for hop in hops for j in range(1, FAN)]

    ctx, me = lax.axis_index("ctx"), lax.axis_index("exp")
    side = lax.rem(ctx, 2)
    pair = ctx // 2
    partner = ctx + 1 - 2 * side
    low = side == 0

    def load(which, g):
        hbm, vmem = ((step_hbm, step_bf), (grad_hbm, grad_bf), (input_hbm, input_bf))[which]
        cols = pl.ds(g * width, width)
        return pltpu.make_async_copy(hbm.at[:, cols], vmem.at[:, cols], load_sem.at[which, g])

    for g in range(groups):
        load(0, g).start()
        load(1, g).start()
    for g in range(groups):
        load(2, g).start()

    barrier = pltpu.get_barrier_semaphore()
    count = 1 + (n_exp - 1)
    pl.semaphore_signal(barrier, inc=1, device_id=(partner, me), device_id_type=MESH)
    for other in range(1, n_exp):
        pl.semaphore_signal(
            barrier, inc=1, device_id=(ctx, lax.rem(me + other, n_exp)), device_id_type=MESH
        )
    for hop in distances:

        @pl.when(pair + hop < pairs)
        def _():
            pl.semaphore_signal(barrier, inc=1, device_id=(ctx + 2 * hop, me), device_id_type=MESH)

        @pl.when(pair >= hop)
        def _():
            pl.semaphore_signal(barrier, inc=1, device_id=(ctx - 2 * hop, me), device_id_type=MESH)

        count = count + jnp.where(pair + hop < pairs, 1, 0) + jnp.where(pair >= hop, 1, 0)

    def repeat(source, target):
        for start in range(0, rows, LANES):
            turned = source[:, start : start + LANES]
            for lane in range(LANES):
                target[start + lane] = jnp.broadcast_to(
                    turned[:, lane : lane + 1], (states, LANES)
                )

    repeat(out_ref, out_rep)
    for g in range(groups):
        for h in range(2):
            at = g * width + h * half
            rate2[g, h] = rate_ref[:, at : at + half] * LOG2E

    def rates(g):
        per_half = TILES // 2
        return [
            rate2[g, w // per_half, :, (w % per_half) * LANES : (w % per_half + 1) * LANES]
            for w in range(TILES)
        ]

    def row(ref, at, tile, sub):
        once = ref[at, tile, pl.ds(sub, 8, stride=0), :]
        return jnp.concatenate([once] * (states // 8), axis=0)

    def columns(g, w):
        return pl.ds(g * width + w * LANES, LANES)

    def first_sweep(g):
        load(0, g).wait()
        load(1, g).wait()
        cols = pl.ds(g * width, width)

        def widen(b, total):
            block = pl.ds(pl.multiple_of(b * WIDE, WIDE), WIDE)
            step = step_bf[block, cols].astype(jnp.float32)
            grad = grad_bf[block, cols].astype(jnp.float32)
            for k in range(WIDE // 8):
                for w in range(TILES):
                    at, lanes = g * TILES + w, slice(w * LANES, (w + 1) * LANES)
                    step_f[at, b * (WIDE // 8) + k] = step[8 * k : 8 * k + 8, lanes]
                    grad_f[at, b * (WIDE // 8) + k] = grad[8 * k : 8 * k + 8, lanes]
                total = total + step[8 * k : 8 * k + 8]
            return total

        total = lax.fori_loop(0, rows // WIDE, widen, jnp.zeros((8, width), jnp.float32))
        rate = rates(g)

        def sweep(k, carry):
            carry = list(carry)
            b = blocks - 1 - k
            for i in range(BLOCK - 1, -1, -1):
                tile, sub = b * (BLOCK // 8) + i // 8, i % 8
                out = out_rep[b * BLOCK + i]
                for w in range(TILES):
                    step = row(step_f, g * TILES + w, tile, sub)
                    grad = row(grad_f, g * TILES + w, tile, sub)
                    factor = jnp.exp2(step * rate[w])
                    decays[g, b * BLOCK + i, :, w * LANES : (w + 1) * LANES] = factor
                    carry[w] = factor * (out * grad + carry[w])
            return tuple(carry)

        zero = jnp.zeros((states, LANES), jnp.float32)
        carry = lax.fori_loop(0, blocks, sweep, (zero,) * TILES)
        reach = jnp.broadcast_to(jnp.sum(total, axis=0, keepdims=True), (8, width))
        per_half = TILES // 2
        for w in range(TILES):
            lanes = slice((w % per_half) * LANES, (w % per_half + 1) * LANES)
            summary[g, w // per_half, :states, lanes] = carry[w]
        for h in range(2):
            summary[g, h, states:, :] = reach[:, h * half : (h + 1) * half]

    def copy_a(g):
        return pltpu.make_async_remote_copy(
            src_ref=summary.at[g, 1 - side], dst_ref=got_a.at[g],
            send_sem=a_sem.at[0, g], recv_sem=a_sem.at[1, g],
            device_id=(partner, me), device_id_type=MESH,
        )

    def copy_b(g, k, j):
        slot = k * (FAN - 1) + j - 1
        return pltpu.make_async_remote_copy(
            src_ref=window.at[g, k], dst_ref=got_b.at[g, slot],
            send_sem=b_sem.at[0, g, slot], recv_sem=b_sem.at[1, g, slot],
            device_id=(ctx - 2 * j * hops[k], me), device_id_type=MESH,
        )

    def copy_c(g):
        return pltpu.make_async_remote_copy(
            src_ref=give.at[g], dst_ref=got_c.at[g],
            send_sem=c_sem.at[0, g], recv_sem=c_sem.at[1, g],
            device_id=(partner, me), device_id_type=MESH,
        )

    def both_sides(g):
        own, other = summary[g, side], got_a[g]
        return jnp.where(low, own, other), jnp.where(low, other, own)

    def decay(rate, reach):
        return jnp.exp2(rate * jnp.concatenate([reach] * (states // 8), axis=0))

    def send_b(g, k):
        for j in range(1, FAN):

            @pl.when(pair >= j * hops[k])
            def _():
                copy_b(g, k, j).start()

    def finish(g):
        first, second = both_sides(g)
        entering = incoming_e[g, :states]
        low_value = second[:states] + decay(rate2[g, side], second[states:]) * entering
        keep[g] = jnp.where(low, low_value, entering)
        give[g] = jnp.where(low, entering, low_value)
        copy_c(g).start()

    def stage(g, s):
        if s == 0:
            copy_a(g).start()
            return
        if s == 1:
            copy_a(g).wait_recv()
            first, second = both_sides(g)
            rate = rate2[g, side]
            window[g, 0, :states] = first[:states] + decay(rate, first[states:]) * second[:states]
            window[g, 0, states:] = first[states:] + second[states:]
            incoming_e[g] = jnp.zeros((states + 8, half), jnp.float32)
            if hops:
                send_b(g, 0)
            else:
                finish(g)
            return
        k = s - 2
        rate = rate2[g, side]

        for j in range(1, FAN):

            @pl.when(pair + j * hops[k] < pairs)
            def _():
                copy_b(g, k, j).wait_recv()
                entering, got = incoming_e[g], got_b[g, k * (FAN - 1) + j - 1]
                incoming_e[g, :states] = (
                    entering[:states] + decay(rate, entering[states:]) * got[:states]
                )
                incoming_e[g, states:] = entering[states:] + got[states:]

        if k + 1 < len(hops):
            mine, entering = window[g, 0], incoming_e[g]
            window[g, k + 1, :states] = (
                mine[:states] + decay(rate, mine[states:]) * entering[:states]
            )
            window[g, k + 1, states:] = mine[states:] + entering[states:]
            send_b(g, k + 1)
        else:
            finish(g)

    stages = 2 + len(hops)
    done = [0] * groups

    def advance(g, limit):
        while done[g] < min(limit, stages):
            stage(g, done[g])
            done[g] += 1

    lane_index = lax.broadcasted_iota(jnp.int32, (states, LANES), 1)

    def weigh_inputs(g):
        load(2, g).wait()
        cols = pl.ds(g * width, width)

        def widen(b, _):
            block = pl.ds(pl.multiple_of(b * WIDE, WIDE), WIDE)
            part = input_bf[block, cols].astype(jnp.float32)
            for k in range(WIDE // 8):
                tile = b * (WIDE // 8) + k
                for w in range(TILES):
                    at, lanes = g * TILES + w, slice(w * LANES, (w + 1) * LANES)
                    x_f[at, tile] = part[8 * k : 8 * k + 8, lanes] * step_f[at, tile]
            return 0

        lax.fori_loop(0, rows // WIDE, widen, 0)

    def second_sweep(g):
        copy_c(g).wait_recv()
        mine, other = keep[g], got_c[g]
        halves = (jnp.where(low, mine, other), jnp.where(low, other, mine))
        per_half = TILES // 2
        carry = tuple(
            halves[w // per_half][:, (w % per_half) * LANES : (w % per_half + 1) * LANES]
            for w in range(TILES)
        )
        last = g == groups - 1
        gain = [gain_ref[:, columns(g, w)] for w in range(TILES)]

        def sweep(q, k, state):
            carry, sums = list(state[0]), state[1]
            per_section = section // BLOCK
            b = (q + 1) * per_section - 1 - k
            for i in range(BLOCK - 1, -1, -1):
                tile, sub = b * (BLOCK // 8) + i // 8, i % 8
                at = b * BLOCK + i
                out, inn = out_rep[at], in_rep[at]
                products = None
                for w in range(TILES):
                    grad = row(grad_f, g * TILES + w, tile, sub)
                    x = row(x_f, g * TILES + w, tile, sub)
                    adjoint = out * grad + carry[w]
                    weighted = inn * adjoint
                    folded = weighted[:8]
                    for s in range(8, states, 8):
                        folded = folded + weighted[s : s + 8]
                    transposer[w, 8 * i : 8 * i + 8, :] = folded
                    product = adjoint * x
                    products = product if products is None else products + product
                    carry[w] = decays[g, at, :, w * LANES : (w + 1) * LANES] * adjoint
                if g > 0:
                    products = products + partial[at]
                if last:
                    summed = jnp.sum(products, axis=1, keepdims=True)
                    sums = jnp.where(lane_index == k_lane(b, i, q), summed, sums)
                else:
                    partial[at] = products
            for w in range(TILES):
                results = []
                for h in range(BLOCK // 8):
                    tile = b * (BLOCK // 8) + h
                    total = transposer[w, pl.ds(64 * h, 8, stride=8), :]
                    for s in range(1, 8):
                        total = total + transposer[w, pl.ds(64 * h + s, 8, stride=8), :]
                    results.append(
                        step_f[g * TILES + w, tile] * total
                        + gain[w] * grad_f[g * TILES + w, tile]
                    )
                dx_bf[pl.ds(pl.multiple_of(b * BLOCK, BLOCK), BLOCK), columns(g, w)] = (
                    jnp.concatenate(results, axis=0).astype(jnp.bfloat16)
                )
            return tuple(carry), sums

        def k_lane(b, i, q):
            return b * BLOCK + i - q * section

        zero = jnp.zeros((states, LANES), jnp.float32)
        if last:
            for q in range(n_exp - 1, -1, -1):
                carry, sums = lax.fori_loop(
                    0, section // BLOCK, functools.partial(sweep, q), (carry, zero)
                )
                share[q] = sums * scale

                @pl.when(me != q)
                def _():
                    copy_share(q).start()
        else:

            def all_rows(k, state):
                carry, _ = sweep_any(k, state)
                return carry, state[1]

            def sweep_any(k, state):
                b = blocks - 1 - k
                per_section = section // BLOCK
                return sweep(n_exp - 1, (n_exp * per_section - 1) - b, state)

            carry, _ = lax.fori_loop(0, blocks, all_rows, (carry, jnp.zeros((8, LANES), jnp.float32)))
        store(g).start()

    def store(g):
        cols = pl.ds(g * width, width)
        return pltpu.make_async_copy(dx_bf.at[:, cols], dx_hbm.at[:, cols], store_sem.at[g])

    def copy_share(q):
        return pltpu.make_async_remote_copy(
            src_ref=share.at[q], dst_ref=got_share.at[me],
            send_sem=r_sem.at[0, q], recv_sem=r_sem.at[1, me],
            device_id=(ctx, q), device_id_type=MESH,
        )

    for g in range(groups):
        first_sweep(g)
        if g == 0:
            pl.semaphore_wait(barrier, count)
        advance(g, 1)
        if g >= 2:
            advance(g - 2, 2)
    repeat(in_ref, in_rep)
    advance(0, 3)
    for g in range(groups):
        weigh_inputs(g)
    for g in range(1, groups):
        advance(g, 2)
    advance(min(1, groups - 1), 3)
    for g in range(groups):
        for later in range(g, groups if g > 0 else 1):
            advance(later, stages)
        second_sweep(g)

    total = share[me]
    for q in range(n_exp):

        @pl.when(me != q)
        def _():
            pltpu.make_async_remote_copy(
                src_ref=share.at[q], dst_ref=got_share.at[q],
                send_sem=r_sem.at[0, q], recv_sem=r_sem.at[1, q],
                device_id=(ctx, q), device_id_type=MESH,
            ).wait_recv()

    for other in range(1, n_exp):
        total = total + got_share[lax.rem(me + other, n_exp)]
    db_ref[...] = total[:, :section]

    for q in range(n_exp):

        @pl.when(me != q)
        def _():
            copy_share(q).wait_send()

    for g in range(groups):
        store(g).wait()
        copy_a(g).wait_send()
        copy_c(g).wait_send()
        for k, hop in enumerate(hops):
            for j in range(1, FAN):

                @pl.when(pair >= j * hop)
                def _():
                    copy_b(g, k, j).wait_send()


def shards(scan_grad, step_size, scan_input, state_in, state_out, decay_rate, skip_gain):
    n_ctx, n_exp = lax.axis_size("ctx"), lax.axis_size("exp")
    rows, channels = scan_grad.shape
    states = state_in.shape[1]
    width = TILES * LANES
    groups, half = channels // width, width // 2
    hops = max(1, len(steps_over(n_ctx // 2)))
    slots = hops * (FAN - 1)
    f32, bf16 = jnp.float32, jnp.bfloat16
    any_spec = pl.BlockSpec(memory_space=pl.ANY)
    vmem = pl.BlockSpec(memory_space=pltpu.VMEM)
    work = rows * channels * states
    return pl.pallas_call(
        functools.partial(kernel, n_ctx, n_exp, 1.0 / math.sqrt(channels * n_exp)),
        out_shape=(
            jax.ShapeDtypeStruct((rows, channels), bf16),
            jax.ShapeDtypeStruct((states, rows // n_exp), f32),
        ),
        in_specs=[any_spec, any_spec, any_spec, vmem, vmem, vmem, vmem],
        out_specs=(any_spec, vmem),
        scratch_shapes=[
            pltpu.VMEM((rows, channels), bf16),
            pltpu.VMEM((rows, channels), bf16),
            pltpu.VMEM((rows, channels), bf16),
            pltpu.VMEM((rows, channels), bf16),
            pltpu.VMEM((channels // LANES, rows // 8, 8, LANES), f32),
            pltpu.VMEM((channels // LANES, rows // 8, 8, LANES), f32),
            pltpu.VMEM((channels // LANES, rows // 8, 8, LANES), f32),
            pltpu.VMEM((rows, states, LANES), f32),
            pltpu.VMEM((rows, states, LANES), f32),
            pltpu.VMEM((rows, states, LANES), f32),
            pltpu.VMEM((TILES, 8 * BLOCK, LANES), f32),
            pltpu.VMEM((groups, rows, states, width), f32),
            pltpu.VMEM((groups, 2, states, half), f32),
            pltpu.VMEM((groups, 2, states + 8, half), f32),
            pltpu.VMEM((groups, states + 8, half), f32),
            pltpu.VMEM((groups, hops, states + 8, half), f32),
            pltpu.VMEM((groups, slots, states + 8, half), f32),
            pltpu.VMEM((groups, states + 8, half), f32),
            pltpu.VMEM((groups, states, half), f32),
            pltpu.VMEM((groups, states, half), f32),
            pltpu.VMEM((groups, states, half), f32),
            pltpu.VMEM((n_exp, states, LANES), f32),
            pltpu.VMEM((n_exp, states, LANES), f32),
            pltpu.SemaphoreType.DMA((3, groups)),
            pltpu.SemaphoreType.DMA((groups,)),
            pltpu.SemaphoreType.DMA((2, groups)),
            pltpu.SemaphoreType.DMA((2, groups, slots)),
            pltpu.SemaphoreType.DMA((2, groups)),
            pltpu.SemaphoreType.DMA((2, n_exp)),
        ],
        compiler_params=pltpu.CompilerParams(
            collective_id=0, has_side_effects=True, vmem_limit_bytes=62 * 1024 * 1024
        ),
        cost_estimate=pl.CostEstimate(
            flops=14 * work, bytes_accessed=8 * rows * channels, transcendentals=2 * work
        ),
    )(
        scan_grad, step_size, scan_input, state_in.T, state_out.T, decay_rate,
        skip_gain.reshape(1, channels),
    )


def solution(mesh):
    in_specs = (
        P("ctx", "exp"),
        P("ctx", "exp"),
        P("ctx", "exp"),
        P("ctx", None),
        P("ctx", None),
        P(None, "exp"),
        P("exp"),
    )
    out_specs = (P("ctx", "exp"), P(None, ("ctx", "exp")))
    return jax.shard_map(shards, mesh=mesh, in_specs=in_specs, out_specs=out_specs, check_vma=False)
```
